32 devices in a mesh: section: 4 (over z), row: 2 (over y), col: 4 (over x, core).
Axes of the slice: x: 2, y: 2, z: 4, core: 2. Of those that a mesh axis runs over, the one named last changes fastest.
Arguments:
- x_fwd: bfloat16 [1024, 12288], P('section', 'row'), may hold values from -6 to 6
- dy_bwd: bfloat16 [1024, 12288], P(('section', 'row'), 'col'), may hold values from -6 to 6
- w_blocks: bfloat16 [4, 2, 4, 460, 128, 128], P('section', 'row', 'col'), may hold values from -0.09375 to 0.09375
- blk_row: int32 [4, 2, 4, 460], P('section', 'row', 'col'), may hold values from 0 to 47, as said below
- blk_col: int32 [4, 2, 4, 460], P('section', 'row', 'col'), may hold values from 0 to 23, as said below
- blk_count: int32 [4, 2, 4], P('section', 'row', 'col'), may hold values from 230 to 460, as said below
- tok_count: int32 [4, 2], P('section'), may hold values from 64 to 256, as said below
- owner_order: int32 [4, 16], P('section'), may hold values from 0 to 15, each once within a row
Outputs:
- y_next: bfloat16 [1024, 12288], P(('section', 'row', 'col'))
- dx_section: bfloat16 [1024, 12288], P(('section', 'row', 'col'))
The draws below stay inside these ranges and needn't reach their ends.
Inputs may be any that keep to these rules, and one draw needn't show every extreme that they name: At each grid position the slots below blk_count name distinct block positions (blk_row, blk_col); the other slots name arbitrary positions. `blk_col`: see blk_row. `blk_count`: some grid position of every draw holds exactly 460 live slots. `tok_count`: index 0 counts the forward micro-batch, index 1 the backward one; valid tokens come first; some entry of every draw equals 256. `owner_order`: each section's row is a permutation.
All inputs are finite; a program needn't handle non-finite values.
Results may differ from the reference program's by a relative error of at most 0.015.
Values may be sent and summed in bfloat16 or wider, within the bound.
No kernel may reach another device: no remote copies, remote signals or barrier semaphores. Data moves between devices by JAX's collectives and lax.ppermute only.
A program may use at most 192 MiB of HBM per device.

```python
import jax
import jax.numpy as jnp
from jax import lax

DMODEL = 12288
DIN = 12288
BLK = 128
TOK = 256
NBI = 96
NBO = 96
BR = 48
BC = 24
POS = 1152
CAP = 460
NRB = 16
RB = 16
TOKENS = 1024
N_SECTION = 4
N_ROW = 2
N_COL = 4


def pattern_lists(key):
    key_count, key_pick, key_order = jax.random.split(jax.random.fold_in(key, 7), 3)
    grid_shape = (N_SECTION, N_ROW, N_COL)
    device_total = N_SECTION * N_ROW * N_COL
    counts = jax.random.randint(key_count, grid_shape, POS // 5, 2 * POS // 5 + 1)
    chosen = jax.random.randint(key_pick, (), 0, device_total)
    position = jnp.arange(device_total).reshape(grid_shape)
    counts = jnp.where(position == chosen, CAP, counts).astype(jnp.int32)
    scores = jax.random.randint(key_order, grid_shape + (POS,), 0, 2 ** 20) * POS + jnp.arange(POS)
    shuffled = jnp.argsort(scores, axis=-1)[..., :CAP].astype(jnp.int32)
    return (counts, (shuffled // BC).astype(jnp.int32), (shuffled % BC).astype(jnp.int32))


def draw_blk_row(key, part):
    return pattern_lists(key)[1]


def draw_blk_col(key, part):
    return pattern_lists(key)[2]


def draw_blk_count(key, part):
    return pattern_lists(key)[0]


def draw_tok_count(key, part):
    key_count, key_pick = jax.random.split(jax.random.fold_in(key, 11), 2)
    counts = jax.random.randint(key_count, (N_SECTION, 2), TOK // 4, TOK + 1)
    chosen = jax.random.randint(key_pick, (), 0, 2 * N_SECTION)
    position = jnp.arange(2 * N_SECTION).reshape(N_SECTION, 2)
    return jnp.where(position == chosen, TOK, counts).astype(jnp.int32)


def shard_levels(own_key, extent, pieces, smallest, top_value):
    loudness = 1.0
    for axis_at, parts in pieces:
        draws = jax.random.uniform(jax.random.fold_in(jax.random.fold_in(own_key, 6), axis_at), (parts,), jnp.float32, smallest / len(pieces), top_value / len(pieces))
        loudness = loudness * jnp.repeat(jnp.exp(draws), extent[axis_at] // parts).reshape((-1,) + (1,) * (len(extent) - 1 - axis_at))
    return loudness


def centred(own_key, shape, deviation, bound, shards=(), dtype=jnp.bfloat16):
    entries = jax.random.normal(own_key, shape, jnp.float32) * deviation
    if len(shards) > 0:
        entries = shard_levels(own_key, shape, shards, -0.22, 0.18) * entries
    return jnp.clip(entries, min=-bound, max=bound).astype(dtype)


def setup_inputs(seed: int = 0) -> dict:
    key_of = jax.random.split(jax.random.key(seed), 9)
    return {
        "x_fwd": centred(key_of[0], (TOKENS, DIN), 1.0, 6.0, ((0, 4), (1, 2))),
        "dy_bwd": centred(key_of[1], (TOKENS, DMODEL), 1.0, 6.0, ((0, 8), (1, 4))),
        "w_blocks": centred(key_of[2], (N_SECTION, N_ROW, N_COL, CAP, BLK, BLK), (3 * DIN // 10) ** -0.5, 0.09375, ((0, 4), (1, 2), (2, 4))),
        "blk_row": draw_blk_row(jax.random.fold_in(key_of[8], 71), 0),
        "blk_col": draw_blk_col(jax.random.fold_in(key_of[8], 71), 0),
        "blk_count": draw_blk_count(jax.random.fold_in(key_of[8], 71), 0),
        "tok_count": draw_tok_count(jax.random.fold_in(key_of[8], 71), 0),
        "owner_order": jax.vmap(lambda own: jax.random.permutation(own, NRB))(jax.random.split(key_of[7], N_SECTION)).reshape((N_SECTION, NRB)).astype(jnp.int32),
    }


def section_pass(inputs):
    x_section, dy_section, w_section, row_slots, col_slots, live_count, tok_limit, owner_rows = inputs
    live = (jnp.arange(CAP)[None, None, :] < live_count[:, :, None]).astype(jnp.float32)
    global_rows = jnp.arange(N_ROW)[:, None, None] * BR + row_slots
    global_cols = jnp.arange(N_COL)[None, :, None] * BC + col_slots
    w_live = w_section.astype(jnp.float32) * live[:, :, :, None, None]
    positions = jnp.arange(TOK)
    keep_fwd = (positions < tok_limit[0]).astype(jnp.float32)
    keep_bwd = (positions < tok_limit[1]).astype(jnp.float32)

    x_blocks = (x_section.astype(jnp.float32) * keep_fwd[:, None]).reshape(TOK, NBI, BLK)
    x_slots = jnp.take(x_blocks, global_rows.reshape(-1), axis=1).reshape(TOK, N_ROW, N_COL * CAP, BLK)
    products = jnp.einsum("trkb,rkbc->trkc", x_slots, w_live.reshape(N_ROW, N_COL * CAP, BLK, BLK),
                          precision=lax.Precision.HIGHEST)
    row_index = jnp.arange(N_ROW)[:, None]
    partial_value = jnp.zeros((TOK, N_ROW, NBO, BLK), jnp.float32).at[
        :, row_index, global_cols.reshape(N_ROW, N_COL * CAP)].add(products)
    rounded = lax.optimization_barrier(partial_value.astype(jnp.bfloat16)).astype(jnp.float32)
    forward = jnp.sum(rounded, axis=1).reshape(TOK, DMODEL).astype(jnp.bfloat16)
    forward = forward.reshape(NRB, RB, DMODEL)[owner_rows].reshape(TOK, DMODEL)

    dy_blocks = (dy_section.astype(jnp.float32) * keep_bwd[:, None]).reshape(TOK, NBO, BLK)
    cols_by_col = jnp.transpose(global_cols, (1, 0, 2)).reshape(N_COL, N_ROW * CAP)
    rows_by_col = jnp.transpose(global_rows * jnp.ones_like(global_cols), (1, 0, 2)).reshape(N_COL, N_ROW * CAP)
    w_by_col = jnp.transpose(w_live, (1, 0, 2, 3, 4)).reshape(N_COL, N_ROW * CAP, BLK, BLK)
    dy_slots = jnp.take(dy_blocks, cols_by_col.reshape(-1), axis=1).reshape(TOK, N_COL, N_ROW * CAP, BLK)
    back_products = jnp.einsum("tckn,ckmn->tckm", dy_slots, w_by_col, precision=lax.Precision.HIGHEST)
    col_index = jnp.arange(N_COL)[:, None]
    back_partial = jnp.zeros((TOK, N_COL, NBI, BLK), jnp.float32).at[
        :, col_index, rows_by_col].add(back_products)
    back_rounded = lax.optimization_barrier(back_partial.astype(jnp.bfloat16)).astype(jnp.float32)
    backward = jnp.sum(back_rounded, axis=1).reshape(TOK, DIN).astype(jnp.bfloat16)
    return forward, backward


def reference(x_fwd, dy_bwd, w_blocks, blk_row, blk_col, blk_count, tok_count, owner_order):
    stacked = (x_fwd.reshape(N_SECTION, TOK, DIN), dy_bwd.reshape(N_SECTION, TOK, DMODEL), w_blocks,
               blk_row, blk_col, blk_count, tok_count, owner_order)
    forward, backward = lax.map(section_pass, stacked)
    shifted = jnp.concatenate([jnp.zeros((1, TOK, DMODEL), jnp.bfloat16), forward[:-1]], axis=0)
    return shifted.reshape(TOKENS, DMODEL), backward.reshape(TOKENS, DIN)
```

```python
import functools

import jax
import jax.numpy as jnp
from jax import lax
from jax.experimental import pallas as pl
from jax.experimental.pallas import tpu as pltpu
from jax.sharding import PartitionSpec as P

F_CHUNKS = (6, 6)
B_CHUNKS = (6, 6, 6, 6)

VMEM = pl.BlockSpec(memory_space=pltpu.VMEM)
SMEM = pl.BlockSpec(memory_space=pltpu.SMEM)
ANY = pl.BlockSpec(memory_space=pl.ANY)
PARAMS = pltpu.CompilerParams(vmem_limit_bytes=40 * 2**20)


def resident(x):
    return pltpu.with_memory_space_constraint(x, pltpu.VMEM)


def prep_kernel(owned, count, row, col, order, w_hbm, x_hbm, w_out, x_out, slot_of, w_sem, x_sem):
    cap = w_hbm.shape[0]
    block_cols = slot_of.shape[1]
    w_copy = pltpu.make_async_copy(w_hbm, w_out.at[pl.ds(0, cap)], w_sem)
    w_copy.start()
    r, c = lax.axis_index("row"), lax.axis_index("col")
    block = x_hbm.shape[0] // order.shape[0]
    per_owner = owned // block
    copies = []
    at = 0
    for dr in range(2):
        for dc in range(4):
            first = ((r ^ dr) * 4 + (c ^ dc)) * per_owner
            for b in range(per_owner):
                source = pl.multiple_of(order[first + b] * block, block)
                copies.append(
                    pltpu.make_async_copy(
                        x_hbm.at[pl.ds(source, block)], x_out.at[pl.ds(at, block)], x_sem.at[len(copies)]
                    )
                )
                copies[-1].start()
                at += block
    w_out[cap] = jnp.zeros(w_out.shape[1:], w_out.dtype)

    @pl.loop(0, slot_of.shape[0])
    def _(i):
        for j in range(block_cols):
            slot_of[i, j] = cap

    live = count[0]

    @pl.loop(0, live)
    def _(k):
        slot_of[row[k], col[k]] = k

    for copy in copies:
        copy.wait()
    w_copy.wait()


def prep(owned, block_cols, count, row, col, order, weights, x):
    cap, size, _ = weights.shape
    block_rows = x.shape[1] // size
    return pl.pallas_call(
        functools.partial(prep_kernel, owned),
        out_shape=(
            pltpu.VMEM((cap + 1, size, size), weights.dtype),
            pltpu.VMEM(x.shape, x.dtype),
            jax.ShapeDtypeStruct((block_rows, block_cols), jnp.int32),
        ),
        in_specs=[SMEM, SMEM, SMEM, SMEM, ANY, ANY],
        out_specs=(VMEM, VMEM, SMEM),
        scratch_shapes=[pltpu.SemaphoreType.DMA, pltpu.SemaphoreType.DMA((order.shape[0],))],
        compiler_params=PARAMS,
    )(count, row, col, order, weights, x)


def forward_kernel(first, slot_of, x, w, keep, send):
    half = keep.shape[0]
    for j in range(keep.shape[1] // 256):
        rhs = jnp.concatenate(
            [
                jnp.concatenate(
                    [w[slot_of[i, 2 * (first + j)]], w[slot_of[i, 2 * (first + j) + 1]]], axis=1
                )
                for i in range(slot_of.shape[0])
            ],
            axis=0,
        )
        part = jnp.dot(x[...], rhs, preferred_element_type=jnp.float32).astype(keep.dtype)
        keep[:, j * 256 : (j + 1) * 256] = part[:half]
        send[:, j * 256 : (j + 1) * 256] = part[half:]


def forward(first, pairs, slot_of, x, w):
    shape = jax.ShapeDtypeStruct((x.shape[0] // 2, pairs * 256), x.dtype)
    return pl.pallas_call(
        functools.partial(forward_kernel, first),
        out_shape=(shape, shape),
        in_specs=[SMEM, VMEM, VMEM],
        out_specs=(VMEM, VMEM),
        compiler_params=PARAMS,
        cost_estimate=pl.CostEstimate(
            flops=2 * x.shape[0] * x.shape[1] * pairs * 256, bytes_accessed=2**20, transcendentals=0
        ),
    )(slot_of, resident(x), resident(w))


def order_grad_kernel(own, other, out, sems):
    c = lax.axis_index("col")
    rows = own.shape[0] // 4
    copies = []
    for dk in range(2):
        for dx in range(2):
            for source in (own, other):
                at = pl.multiple_of((c ^ (2 * dx + dk)) * rows, rows)
                copies.append(
                    pltpu.make_async_copy(
                        source.at[pl.ds(at, rows)], out.at[pl.ds(len(copies) * rows, rows)], sems.at[len(copies)]
                    )
                )
                copies[-1].start()
    for copy in copies:
        copy.wait()


def order_grad(own, other):
    rows, width = own.shape
    return pl.pallas_call(
        order_grad_kernel,
        out_shape=pltpu.VMEM((2 * rows, width), own.dtype),
        in_specs=[ANY, ANY],
        out_specs=VMEM,
        scratch_shapes=[pltpu.SemaphoreType.DMA((8,))],
        compiler_params=PARAMS,
    )(own, other)


def backward_kernel(first, slot_of, dy, w, keep, send):
    half = keep.shape[0]
    for i in range(keep.shape[1] // 256):
        rhs = jnp.concatenate(
            [
                jnp.concatenate(
                    [w[slot_of[2 * (first + i), j]], w[slot_of[2 * (first + i) + 1, j]]], axis=0
                )
                for j in range(slot_of.shape[1])
            ],
            axis=1,
        )
        part = lax.dot_general(
            dy[...], rhs, (((1,), (1,)), ((), ())), preferred_element_type=jnp.float32
        ).astype(keep.dtype)
        keep[:, i * 256 : (i + 1) * 256] = part[:half]
        send[:, i * 256 : (i + 1) * 256] = part[half:]


def backward(first, pairs, slot_of, dy, w):
    shape = jax.ShapeDtypeStruct((dy.shape[0] // 2, pairs * 256), dy.dtype)
    return pl.pallas_call(
        functools.partial(backward_kernel, first),
        out_shape=(shape, shape),
        in_specs=[SMEM, VMEM, VMEM],
        out_specs=(VMEM, VMEM),
        compiler_params=PARAMS,
        cost_estimate=pl.CostEstimate(
            flops=2 * dy.shape[0] * dy.shape[1] * pairs * 256, bytes_accessed=2**20, transcendentals=0
        ),
    )(slot_of, resident(dy), resident(w))


def sum_forward_kernel(block, order, limits, keep, received, *outs):
    r, c = lax.axis_index("row"), lax.axis_index("col")
    rows = outs[0].shape[0]
    per_owner = rows // block
    for dc, out in enumerate(outs):
        first = (r * 4 + (c ^ dc)) * per_owner
        for b in range(per_owner):
            at = dc * rows + b * block
            total = keep[at : at + block].astype(jnp.float32) + received[at : at + block].astype(jnp.float32)
            token = order[first + b] * block + lax.broadcasted_iota(jnp.int32, total.shape, 0)
            out[b * block : (b + 1) * block] = jnp.where(token < limits[0], total, 0.0).astype(out.dtype)


def sum_forward(block, order, limits, keep, received):
    rows, width = keep.shape
    return pl.pallas_call(
        functools.partial(sum_forward_kernel, block),
        out_shape=(jax.ShapeDtypeStruct((rows // 4, width), keep.dtype),) * 4,
        in_specs=[SMEM, SMEM, VMEM, VMEM],
        out_specs=(VMEM,) * 4,
        compiler_params=PARAMS,
    )(order, limits, keep, received)


def place_forward_kernel(*refs):
    pieces, out, sems = refs[:-2], refs[-2], refs[-1]
    c = lax.axis_index("col")
    width = out.shape[1] // 4
    copies = []
    for dc in range(4):
        at = (c ^ dc) * width
        for piece in pieces[dc::4]:
            copies.append(
                pltpu.make_async_copy(
                    piece, out.at[:, pl.ds(pl.multiple_of(at, 128), piece.shape[1])], sems.at[len(copies)]
                )
            )
            copies[-1].start()
            at += piece.shape[1]
    for copy in copies:
        copy.wait()


def place_forward(pieces):
    rows = pieces[0].shape[0]
    width = sum(piece.shape[1] for piece in pieces)
    return pl.pallas_call(
        place_forward_kernel,
        out_shape=jax.ShapeDtypeStruct((rows, width), pieces[0].dtype),
        in_specs=[ANY] * len(pieces),
        out_specs=ANY,
        scratch_shapes=[pltpu.SemaphoreType.DMA((len(pieces),))],
        compiler_params=PARAMS,
    )(*pieces)


def place_backward_kernel(limits, *refs):
    pieces, out = refs[:-1], refs[-1]
    r, c = lax.axis_index("row"), lax.axis_index("col")
    rows = out.shape[0]
    width = out.shape[1] // 2
    for dr in range(2):
        at = (r ^ dr) * width
        for piece in pieces[dr::2]:
            token = (r * 4 + c) * rows + lax.broadcasted_iota(jnp.int32, piece.shape, 0)
            value = jnp.where(token < limits[1], piece[...].astype(jnp.float32), 0.0).astype(out.dtype)
            out[:, pl.ds(pl.multiple_of(at, 128), piece.shape[1])] = value
            at += piece.shape[1]


def place_backward(limits, pieces):
    rows = pieces[0].shape[0]
    width = sum(piece.shape[1] for piece in pieces)
    return pl.pallas_call(
        place_backward_kernel,
        out_shape=jax.ShapeDtypeStruct((rows, width), pieces[0].dtype),
        in_specs=[SMEM] + [VMEM] * len(pieces),
        out_specs=VMEM,
        compiler_params=PARAMS,
    )(limits, *pieces)


def swap(x, axis, by):
    return lax.ppermute(x, axis, [(i, i ^ by) for i in range(lax.axis_size(axis))])


def deliver(x, by):
    sections, rows, cols = lax.axis_size("section"), lax.axis_size("row"), lax.axis_size("col")
    at = lambda s, r, c: (s * rows + r) * cols + c
    pairs = [
        (at(s, r, c), at(s + 1, r, c ^ by))
        for s in range(sections - 1)
        for r in range(rows)
        for c in range(cols)
    ]
    return lax.ppermute(x, ("section", "row", "col"), pairs)


def added(a, b):
    return (a.astype(jnp.float32) + b.astype(jnp.float32)).astype(a.dtype)


def grid_2x4(x_fwd, dy_bwd, w_blocks, blk_row, blk_col, blk_count, tok_count, owner_order):
    token_total = x_fwd.shape[0]
    owned = token_total // 8
    slots, size = w_blocks.shape[3], w_blocks.shape[5]
    order = owner_order.reshape(-1)
    limits = tok_count.reshape(2)
    dy_other = swap(dy_bwd, "row", 1)
    w, x, slot_of = prep(
        owned,
        dy_bwd.shape[1] // size,
        blk_count.reshape(1),
        blk_row.reshape(slots),
        blk_col.reshape(slots),
        order,
        w_blocks.reshape(slots, size, size),
        x_fwd,
    )
    pieces = []
    first = 0
    for pairs in F_CHUNKS:
        keep, send = forward(first, pairs, slot_of, x, w)
        first += pairs
        summed = sum_forward(token_total // order.shape[0], order, limits, keep, swap(send, "row", 1))
        pieces += [deliver(summed[by], by) for by in range(4)]
    y_next = place_forward(pieces)

    dy = order_grad(dy_bwd, dy_other)
    pieces = []
    first = 0
    for pairs in B_CHUNKS:
        keep, send = backward(first, pairs, slot_of, dy, w)
        first += pairs
        received = swap(send, "col", 1)
        half = keep.shape[0] // 2
        onward = added(keep[half:], received[half:])
        kept = added(keep[:half], received[:half])
        received = swap(onward, "col", 2)
        onward = added(kept[owned:], received[owned:])
        kept = added(kept[:owned], received[:owned])
        pieces += [kept, swap(onward, "row", 1)]
    dx_section = place_backward(limits, pieces)
    return y_next, dx_section


def passed_along(shard, axis, by):
    length = lax.axis_size(axis)
    pairs = [(i, i + by) for i in range(length) if 0 <= i + by < length]
    return lax.ppermute(shard, axis, pairs)


def any_grid(x_fwd, dy_bwd, w_blocks, blk_row, blk_col, blk_count, tok_count, owner_order):
    row_count = lax.axis_size("row")
    col_count = lax.axis_size("col")
    token_total, in_width = x_fwd.shape
    out_width = dy_bwd.shape[1]
    slot_total = w_blocks.shape[3]
    block_size = w_blocks.shape[5]
    block_rows = in_width // block_size
    block_cols = out_width // block_size
    owned_rows = token_total // (row_count * col_count)
    weights = w_blocks.reshape(slot_total, block_size, block_size)
    live = (jnp.arange(slot_total) < blk_count.reshape(())).astype(weights.dtype)
    dense_blocks = jnp.zeros((block_rows, block_cols, block_size, block_size), weights.dtype)
    dense_blocks = dense_blocks.at[blk_row.reshape(slot_total), blk_col.reshape(slot_total)].add(
        weights * live[:, None, None]
    )
    dense_weight = jnp.transpose(dense_blocks, (0, 2, 1, 3)).reshape(in_width, out_width)
    limits = tok_count.reshape(2)
    block_total = owner_order.shape[1]
    block_length = token_total // block_total
    token_index = (
        owner_order.reshape(block_total)[:, None] * block_length + jnp.arange(block_length)[None, :]
    ).reshape(token_total)
    ordered_rows = jnp.take(x_fwd, token_index, axis=0)
    ordered_rows = jnp.where(
        (token_index < limits[0])[:, None], ordered_rows, jnp.zeros_like(ordered_rows)
    )
    partial_value = jnp.dot(ordered_rows, dense_weight, preferred_element_type=jnp.float32).astype(
        jnp.bfloat16
    )
    outgoing = partial_value.reshape(row_count * col_count, owned_rows, out_width)
    received = lax.all_to_all(outgoing, ("row", "col"), split_axis=0, concat_axis=2, tiled=True)
    summed = received.reshape(owned_rows, row_count, col_count * out_width).astype(jnp.float32)
    forward_act = jnp.sum(summed, axis=1).astype(jnp.bfloat16)
    y_next = passed_along(forward_act, "section", 1)
    grad_rows = dy_bwd.shape[0]
    grad_index = lax.axis_index("row") * grad_rows + jnp.arange(grad_rows)
    grad_kept = jnp.where((grad_index < limits[1])[:, None], dy_bwd, jnp.zeros_like(dy_bwd))
    grad_partial = lax.dot_general(
        lax.all_gather(grad_kept, "row", axis=0, tiled=True),
        dense_weight,
        (((1,), (1,)), ((), ())),
        preferred_element_type=jnp.float32,
    ).astype(jnp.bfloat16)
    grad_outgoing = grad_partial.reshape(row_count * col_count, owned_rows, in_width)
    grad_received = lax.all_to_all(
        grad_outgoing, ("row", "col"), split_axis=0, concat_axis=2, tiled=True
    )
    grad_summed = grad_received.reshape(owned_rows, row_count, col_count, in_width).astype(
        jnp.float32
    )
    dx_section = (
        jnp.sum(grad_summed, axis=2).reshape(owned_rows, row_count * in_width).astype(jnp.bfloat16)
    )
    return (y_next, dx_section)


def solution(mesh):
    small = mesh.shape["row"] == 2 and mesh.shape["col"] == 4
    return jax.shard_map(
        grid_2x4 if small else any_grid,
        mesh=mesh,
        in_specs=(
            P("section", "row"),
            P(("section", "row"), "col"),
            P("section", "row", "col", None, None, None),
            P("section", "row", "col", None),
            P("section", "row", "col", None),
            P("section", "row", "col"),
            P("section", None),
            P("section", None),
        ),
        out_specs=(P(("section", "row", "col"), None), P(("section", "row", "col"), None)),
        check_vma=False,
    )
```

```python
import functools

import jax
import jax.numpy as jnp
from jax import lax
from jax.experimental import pallas as pl
from jax.experimental.pallas import tpu as pltpu
from jax.sharding import PartitionSpec as P

F_PARTS = 2
B_PARTS = 4

VMEM = pl.BlockSpec(memory_space=pltpu.VMEM)
SMEM = pl.BlockSpec(memory_space=pltpu.SMEM)
ANY = pl.BlockSpec(memory_space=pl.ANY)
HBM = pl.BlockSpec(memory_space=pltpu.HBM)
PARAMS = pltpu.CompilerParams(vmem_limit_bytes=16 * 2**20)


def resident(x):
    return pltpu.with_memory_space_constraint(x, pltpu.VMEM)


def in_hbm(x):
    return pltpu.with_memory_space_constraint(x, pltpu.HBM)


def divisor(n, most):
    return max(d for d in range(1, most + 1) if n % d == 0)


def prep_kernel(
    owned, block_rows, block_cols,
    count, row_hbm, col_hbm, order_hbm, w_hbm, x_hbm,
    w_out, x_out, slot_of,
    row, col, order, w_sem, x_sem, list_sem,
):
    cap = w_hbm.shape[0]
    positions = block_rows * block_cols
    lists = [
        pltpu.make_async_copy(source, target, list_sem.at[i])
        for i, (source, target) in enumerate(
            ((order_hbm, order), (row_hbm, row), (col_hbm, col))
        )
    ]
    for copy in lists:
        copy.start()
    w_copy = pltpu.make_async_copy(w_hbm, w_out.at[pl.ds(0, cap)], w_sem)
    w_copy.start()
    w_out[cap] = jnp.zeros(w_out.shape[1:], w_out.dtype)

    @pl.loop(0, positions // block_cols)
    def _(i):
        for j in range(block_cols):
            slot_of[i * block_cols + j] = cap

    lists[0].wait()
    r, c = lax.axis_index("row"), lax.axis_index("col")
    block = x_hbm.shape[0] // order.shape[1]
    per_owner = owned // block
    copies = []
    at = 0
    for dr in range(2):
        for dc in range(4):
            first = ((r ^ dr) * 4 + (c ^ dc)) * per_owner
            for b in range(per_owner):
                source = pl.multiple_of(order[0, first + b] * block, block)
                copies.append(
                    pltpu.make_async_copy(
                        x_hbm.at[pl.ds(source, block)], x_out.at[pl.ds(at, block)], x_sem.at[len(copies)]
                    )
                )
                copies[-1].start()
                at += block
    for copy in lists[1:]:
        copy.wait()
    live = count[0]
    step = divisor(cap, 20)

    @pl.loop(0, cap // step)
    def _(i):
        for j in range(step):
            k = i * step + j
            place = row[0, k] * block_cols + col[0, k]
            slot_of[jnp.where(k < live, place, positions)] = k

    for copy in copies:
        copy.wait()
    w_copy.wait()


def prep(owned, block_cols, count, row, col, order, weights, x):
    cap, size, _ = weights.shape
    block_rows = x.shape[1] // size
    lists = (row, col, order)
    return pl.pallas_call(
        functools.partial(prep_kernel, owned, block_rows, block_cols),
        out_shape=(
            pltpu.VMEM((cap + 1, size, size), weights.dtype),
            pltpu.VMEM(x.shape, x.dtype),
            jax.ShapeDtypeStruct((block_rows * block_cols + 1,), jnp.int32),
        ),
        in_specs=[SMEM] + [HBM] * 5,
        out_specs=(VMEM, VMEM, SMEM),
        scratch_shapes=[pltpu.SMEM(a.shape, a.dtype) for a in lists]
        + [
            pltpu.SemaphoreType.DMA,
            pltpu.SemaphoreType.DMA((order.shape[1],)),
            pltpu.SemaphoreType.DMA((len(lists),)),
        ],
        compiler_params=PARAMS,
    )(count, *[in_hbm(a) for a in (*lists, weights, x)])


def forward_kernel(block, order, limits, slot_of, x, w, *outs):
    r, c = lax.axis_index("row"), lax.axis_index("col")
    rows = x.shape[0]
    half = rows // 2
    per_owner = rows // 8 // block
    size = w.shape[1]
    pair = 2 * size
    tokens = []
    for dr in range(2):
        for dc in range(4):
            for b in range(per_owner):
                first = order[((r ^ dr) * 4 + (c ^ dc)) * per_owner + b] * block
                tokens.append(first + lax.broadcasted_iota(jnp.int32, (block, pair), 0))
    live = jnp.concatenate(tokens, axis=0) < limits[0]
    block_cols = sum(send.shape[1] for send in outs[1::2]) // size
    column = 0
    for keep, send in zip(outs[::2], outs[1::2]):
        for j in range(keep.shape[1] // pair):
            rhs = jnp.concatenate(
                [
                    jnp.concatenate([w[slot_of[i + column]], w[slot_of[i + column + 1]]], axis=1)
                    for i in range(0, slot_of.shape[0] - 1, block_cols)
                ],
                axis=0,
            )
            part = jnp.dot(x[...], rhs, preferred_element_type=jnp.float32)
            part = jnp.where(live, part, 0.0).astype(keep.dtype)
            keep[:, j * pair : (j + 1) * pair] = part[:half]
            send[:, j * pair : (j + 1) * pair] = part[half:]
            column += 2


def forward(block, order, limits, slot_of, x, w, width):
    shape = pltpu.VMEM((x.shape[0] // 2, width // F_PARTS), x.dtype)
    return pl.pallas_call(
        functools.partial(forward_kernel, block),
        out_shape=(shape,) * (2 * F_PARTS),
        in_specs=[SMEM, SMEM, SMEM, VMEM, VMEM],
        out_specs=(VMEM,) * (2 * F_PARTS),
        compiler_params=PARAMS,
        cost_estimate=pl.CostEstimate(flops=1000, bytes_accessed=1000, transcendentals=0),
    )(order, limits, slot_of, resident(x), resident(w))


def backward_kernel(first, slot_of, own, other, w, *refs):
    keep, send, dy = refs[-3:]
    c = lax.axis_index("col")
    owned = own.shape[0] // 4
    size = w.shape[1]
    block_cols = own.shape[1] // size
    at = 0
    for dk in range(2):
        for dx in range(2):
            rows = pl.ds(pl.multiple_of((c ^ (2 * dx + dk)) * owned, owned), owned)
            for source in (own, other):
                dy[at : at + owned] = source[rows]
                at += owned
    half = keep.shape[0]
    pair = 2 * size
    for i in range(keep.shape[1] // pair):
        at = (first + 2 * i) * block_cols
        rhs = jnp.concatenate(
            [
                jnp.concatenate([w[slot_of[at + j]], w[slot_of[at + block_cols + j]]], axis=0)
                for j in range(block_cols)
            ],
            axis=1,
        )
        part = lax.dot_general(
            dy[...], rhs, (((1,), (1,)), ((), ())), preferred_element_type=jnp.float32
        ).astype(keep.dtype)
        keep[:, i * pair : (i + 1) * pair] = part[:half]
        send[:, i * pair : (i + 1) * pair] = part[half:]


def backward(part, slot_of, own, other, w, after):
    block_cols = own.shape[1] // w.shape[1]
    block_rows = slot_of.shape[0] // block_cols
    shape = pltpu.VMEM((own.shape[0], block_rows * w.shape[1] // B_PARTS), own.dtype)
    return pl.pallas_call(
        functools.partial(backward_kernel, part * (block_rows // B_PARTS)),
        out_shape=(shape, shape),
        in_specs=[SMEM, VMEM, VMEM, VMEM] + [ANY] * len(after),
        out_specs=(VMEM, VMEM),
        scratch_shapes=[pltpu.VMEM((2 * own.shape[0], own.shape[1]), own.dtype)],
        compiler_params=PARAMS,
        cost_estimate=pl.CostEstimate(flops=1000, bytes_accessed=1000, transcendentals=0),
    )(slot_of, own, other, resident(w), *after)


def place_forward_kernel(*refs):
    pieces, out, sems = refs[:-2], refs[-2], refs[-1]
    c = lax.axis_index("col")
    width = out.shape[1] // 4
    copies = []
    for dc in range(4):
        at = (c ^ dc) * width
        for piece in pieces[dc::4]:
            copies.append(
                pltpu.make_async_copy(
                    piece, out.at[:, pl.ds(pl.multiple_of(at, 128), piece.shape[1])], sems.at[len(copies)]
                )
            )
            copies[-1].start()
            at += piece.shape[1]
    for copy in copies:
        copy.wait()


def place_forward(pieces):
    rows = pieces[0].shape[0]
    width = sum(piece.shape[1] for piece in pieces)
    return pl.pallas_call(
        place_forward_kernel,
        out_shape=jax.ShapeDtypeStruct((rows, width), pieces[0].dtype),
        in_specs=[ANY] * len(pieces),
        out_specs=ANY,
        scratch_shapes=[pltpu.SemaphoreType.DMA((len(pieces),))],
        compiler_params=PARAMS,
    )(*pieces)


def place_backward_kernel(limits, *refs):
    pieces, out = refs[:-1], refs[-1]
    r, c = lax.axis_index("row"), lax.axis_index("col")
    rows = out.shape[0]
    width = out.shape[1] // 2
    for dr in range(2):
        at = (r ^ dr) * width
        for piece in pieces[dr::2]:
            token = (r * 4 + c) * rows + lax.broadcasted_iota(jnp.int32, piece.shape, 0)
            value = jnp.where(token < limits[1], piece[...].astype(jnp.float32), 0.0).astype(out.dtype)
            out[:, pl.ds(pl.multiple_of(at, 128), piece.shape[1])] = value
            at += piece.shape[1]


def place_backward(limits, pieces):
    rows = pieces[0].shape[0]
    width = sum(piece.shape[1] for piece in pieces)
    return pl.pallas_call(
        place_backward_kernel,
        out_shape=jax.ShapeDtypeStruct((rows, width), pieces[0].dtype),
        in_specs=[SMEM] + [VMEM] * len(pieces),
        out_specs=VMEM,
        compiler_params=PARAMS,
    )(limits, *pieces)


def swap(x, axis, by):
    return lax.ppermute(x, axis, [(i, i ^ by) for i in range(lax.axis_size(axis))])


def added(a, b):
    return (a.astype(jnp.float32) + b.astype(jnp.float32)).astype(a.dtype)


def grid_2x4(x_fwd, dy_bwd, w_blocks, blk_row, blk_col, blk_count, tok_count, owner_order):
    token_total = x_fwd.shape[0]
    owned = token_total // 8
    slots, size = w_blocks.shape[3], w_blocks.shape[5]
    order = owner_order.reshape(-1)
    limits = tok_count.reshape(2)
    block = token_total // order.shape[0]
    dy_other = swap(dy_bwd, "row", 1)
    w, x, slot_of = prep(
        owned,
        dy_bwd.shape[1] // size,
        blk_count.reshape(1),
        blk_row.reshape(1, slots),
        blk_col.reshape(1, slots),
        owner_order,
        w_blocks.reshape(slots, size, size),
        x_fwd,
    )
    parts = forward(block, order, limits, slot_of, x, w, dy_bwd.shape[1])
    keeps, sends = parts[::2], parts[1::2]
    *sends, dy_other = lax.optimization_barrier((*sends, dy_other))

    y_pieces, dx_pieces = [], []
    forward_sums, backward_sums = [], []
    for part in range(B_PARTS):
        after = backward_sums[part - 2 : part - 1] if part >= 2 else []
        if part == B_PARTS - 1:
            after = after + forward_sums[:1]
        keep, send = backward(part, slot_of, dy_bwd, dy_other, w, after)
        if part < F_PARTS:
            summed = added(keeps[part], swap(sends[part], "row", 1))
            forward_sums.append(summed)
            shifted = passed_along(summed, "section", 1)
            here, there = shifted[: 2 * owned], swap(shifted[2 * owned :], "col", 2)
            y_pieces += [here[:owned], swap(here[owned:], "col", 1), there[:owned], swap(there[owned:], "col", 1)]
        received = swap(send, "col", 1)
        half = keep.shape[0] // 2
        onward = added(keep[half:], received[half:])
        backward_sums.append(onward)
        kept = added(keep[:half], received[:half])
        received = swap(onward, "col", 2)
        onward = added(kept[owned:], received[owned:])
        kept = added(kept[:owned], received[:owned])
        dx_pieces += [kept, swap(onward, "row", 1)]
    return place_forward(y_pieces), place_backward(limits, dx_pieces)


def passed_along(shard, axis, by):
    length = lax.axis_size(axis)
    pairs = [(i, i + by) for i in range(length) if 0 <= i + by < length]
    return lax.ppermute(shard, axis, pairs)


def any_grid(x_fwd, dy_bwd, w_blocks, blk_row, blk_col, blk_count, tok_count, owner_order):
    row_count = lax.axis_size("row")
    col_count = lax.axis_size("col")
    token_total, in_width = x_fwd.shape
    out_width = dy_bwd.shape[1]
    slot_total = w_blocks.shape[3]
    block_size = w_blocks.shape[5]
    block_rows = in_width // block_size
    block_cols = out_width // block_size
    owned_rows = token_total // (row_count * col_count)
    weights = w_blocks.reshape(slot_total, block_size, block_size)
    live = (jnp.arange(slot_total) < blk_count.reshape(())).astype(weights.dtype)
    dense_blocks = jnp.zeros((block_rows, block_cols, block_size, block_size), weights.dtype)
    dense_blocks = dense_blocks.at[blk_row.reshape(slot_total), blk_col.reshape(slot_total)].add(
        weights * live[:, None, None]
    )
    dense_weight = jnp.transpose(dense_blocks, (0, 2, 1, 3)).reshape(in_width, out_width)
    limits = tok_count.reshape(2)
    block_total = owner_order.shape[1]
    block_length = token_total // block_total
    token_index = (
        owner_order.reshape(block_total)[:, None] * block_length + jnp.arange(block_length)[None, :]
    ).reshape(token_total)
    ordered_rows = jnp.take(x_fwd, token_index, axis=0)
    ordered_rows = jnp.where(
        (token_index < limits[0])[:, None], ordered_rows, jnp.zeros_like(ordered_rows)
    )
    partial_value = jnp.dot(ordered_rows, dense_weight, preferred_element_type=jnp.float32).astype(
        jnp.bfloat16
    )
    outgoing = partial_value.reshape(row_count * col_count, owned_rows, out_width)
    received = lax.all_to_all(outgoing, ("row", "col"), split_axis=0, concat_axis=2, tiled=True)
    summed = received.reshape(owned_rows, row_count, col_count * out_width).astype(jnp.float32)
    forward_act = jnp.sum(summed, axis=1).astype(jnp.bfloat16)
    y_next = passed_along(forward_act, "section", 1)
    grad_rows = dy_bwd.shape[0]
    grad_index = lax.axis_index("row") * grad_rows + jnp.arange(grad_rows)
    grad_kept = jnp.where((grad_index < limits[1])[:, None], dy_bwd, jnp.zeros_like(dy_bwd))
    grad_partial = lax.dot_general(
        lax.all_gather(grad_kept, "row", axis=0, tiled=True),
        dense_weight,
        (((1,), (1,)), ((), ())),
        preferred_element_type=jnp.float32,
    ).astype(jnp.bfloat16)
    grad_outgoing = grad_partial.reshape(row_count * col_count, owned_rows, in_width)
    grad_received = lax.all_to_all(
        grad_outgoing, ("row", "col"), split_axis=0, concat_axis=2, tiled=True
    )
    grad_summed = grad_received.reshape(owned_rows, row_count, col_count, in_width).astype(
        jnp.float32
    )
    dx_section = (
        jnp.sum(grad_summed, axis=2).reshape(owned_rows, row_count * in_width).astype(jnp.bfloat16)
    )
    return (y_next, dx_section)


def solution(mesh):
    small = mesh.shape["row"] == 2 and mesh.shape["col"] == 4
    return jax.shard_map(
        grid_2x4 if small else any_grid,
        mesh=mesh,
        in_specs=(
            P("section", "row"),
            P(("section", "row"), "col"),
            P("section", "row", "col", None, None, None),
            P("section", "row", "col", None),
            P("section", "row", "col", None),
            P("section", "row", "col"),
            P("section", None),
            P("section", None),
        ),
        out_specs=(P(("section", "row", "col"), None), P(("section", "row", "col"), None)),
        check_vma=False,
    )
```

```python
import functools

import jax
import jax.numpy as jnp
from jax import lax
from jax.experimental import pallas as pl
from jax.experimental.pallas import tpu as pltpu
from jax.sharding import PartitionSpec as P

AFTER = ((), (), ('c0','y0'), ('k2','c1'))
F_PARTS = 2
B_PARTS = 4

VMEM = pl.BlockSpec(memory_space=pltpu.VMEM)
SMEM = pl.BlockSpec(memory_space=pltpu.SMEM)
ANY = pl.BlockSpec(memory_space=pl.ANY)
HBM = pl.BlockSpec(memory_space=pltpu.HBM)
PARAMS = pltpu.CompilerParams(vmem_limit_bytes=16 * 2**20)


def resident(x):
    return pltpu.with_memory_space_constraint(x, pltpu.VMEM)


def in_hbm(x):
    return pltpu.with_memory_space_constraint(x, pltpu.HBM)


def divisor(n, most):
    return max(d for d in range(1, most + 1) if n % d == 0)


def prep_kernel(
    owned, block_rows, block_cols,
    count, row_hbm, col_hbm, order_hbm, w_hbm, x_hbm,
    w_out, x_out, slot_of,
    row, col, order, w_sem, x_sem, list_sem,
):
    cap = w_hbm.shape[0]
    positions = block_rows * block_cols
    lists = [
        pltpu.make_async_copy(source, target, list_sem.at[i])
        for i, (source, target) in enumerate(
            ((order_hbm, order), (row_hbm, row), (col_hbm, col))
        )
    ]
    for copy in lists:
        copy.start()
    w_copy = pltpu.make_async_copy(w_hbm, w_out.at[pl.ds(0, cap)], w_sem)
    w_copy.start()
    w_out[cap] = jnp.zeros(w_out.shape[1:], w_out.dtype)

    @pl.loop(0, positions // block_cols)
    def _(i):
        for j in range(block_cols):
            slot_of[i * block_cols + j] = cap

    lists[0].wait()
    r, c = lax.axis_index("row"), lax.axis_index("col")
    block = x_hbm.shape[0] // order.shape[1]
    per_owner = owned // block
    copies = []
    at = 0
    for dr in range(2):
        for dc in range(4):
            first = ((r ^ dr) * 4 + (c ^ dc)) * per_owner
            for b in range(per_owner):
                source = pl.multiple_of(order[0, first + b] * block, block)
                copies.append(
                    pltpu.make_async_copy(
                        x_hbm.at[pl.ds(source, block)], x_out.at[pl.ds(at, block)], x_sem.at[len(copies)]
                    )
                )
                copies[-1].start()
                at += block
    for copy in lists[1:]:
        copy.wait()
    live = count[0]
    step = divisor(cap, 20)

    @pl.loop(0, cap // step)
    def _(i):
        for j in range(step):
            k = i * step + j
            place = row[0, k] * block_cols + col[0, k]
            slot_of[jnp.where(k < live, place, positions)] = k

    for copy in copies:
        copy.wait()
    w_copy.wait()


def prep(owned, block_cols, count, row, col, order, weights, x):
    cap, size, _ = weights.shape
    block_rows = x.shape[1] // size
    lists = (row, col, order)
    return pl.pallas_call(
        functools.partial(prep_kernel, owned, block_rows, block_cols),
        out_shape=(
            pltpu.VMEM((cap + 1, size, size), weights.dtype),
            pltpu.VMEM(x.shape, x.dtype),
            jax.ShapeDtypeStruct((block_rows * block_cols + 1,), jnp.int32),
        ),
        in_specs=[SMEM] + [HBM] * 5,
        out_specs=(VMEM, VMEM, SMEM),
        scratch_shapes=[pltpu.SMEM(a.shape, a.dtype) for a in lists]
        + [
            pltpu.SemaphoreType.DMA,
            pltpu.SemaphoreType.DMA((order.shape[1],)),
            pltpu.SemaphoreType.DMA((len(lists),)),
        ],
        compiler_params=PARAMS,
    )(count, *[in_hbm(a) for a in (*lists, weights, x)])


def forward_kernel(block, order, limits, slot_of, x, w, *outs):
    r, c = lax.axis_index("row"), lax.axis_index("col")
    rows = x.shape[0]
    half = rows // 2
    per_owner = rows // 8 // block
    size = w.shape[1]
    pair = 2 * size
    tokens = []
    for dr in range(2):
        for dc in range(4):
            for b in range(per_owner):
                first = order[((r ^ dr) * 4 + (c ^ dc)) * per_owner + b] * block
                tokens.append(first + lax.broadcasted_iota(jnp.int32, (block, pair), 0))
    live = jnp.concatenate(tokens, axis=0) < limits[0]
    block_cols = sum(send.shape[1] for send in outs[1::2]) // size
    column = 0
    for keep, send in zip(outs[::2], outs[1::2]):
        for j in range(keep.shape[1] // pair):
            rhs = jnp.concatenate(
                [
                    jnp.concatenate([w[slot_of[i + column]], w[slot_of[i + column + 1]]], axis=1)
                    for i in range(0, slot_of.shape[0] - 1, block_cols)
                ],
                axis=0,
            )
            part = jnp.dot(x[...], rhs, preferred_element_type=jnp.float32)
            part = jnp.where(live, part, 0.0).astype(keep.dtype)
            keep[:, j * pair : (j + 1) * pair] = part[:half]
            send[:, j * pair : (j + 1) * pair] = part[half:]
            column += 2


def forward(block, order, limits, slot_of, x, w, width):
    shape = pltpu.VMEM((x.shape[0] // 2, width // F_PARTS), x.dtype)
    return pl.pallas_call(
        functools.partial(forward_kernel, block),
        out_shape=(shape,) * (2 * F_PARTS),
        in_specs=[SMEM, SMEM, SMEM, VMEM, VMEM],
        out_specs=(VMEM,) * (2 * F_PARTS),
        compiler_params=PARAMS,
        cost_estimate=pl.CostEstimate(flops=1000, bytes_accessed=1000, transcendentals=0),
    )(order, limits, slot_of, resident(x), resident(w))


def backward_kernel(first, slot_of, own, other, w, *refs):
    keep, send, dy = refs[-3:]
    c = lax.axis_index("col")
    owned = own.shape[0] // 4
    size = w.shape[1]
    block_cols = own.shape[1] // size
    at = 0
    for dk in range(2):
        for dx in range(2):
            rows = pl.ds(pl.multiple_of((c ^ (2 * dx + dk)) * owned, owned), owned)
            for source in (own, other):
                dy[at : at + owned] = source[rows]
                at += owned
    half = keep.shape[0]
    pair = 2 * size
    for i in range(keep.shape[1] // pair):
        at = (first + 2 * i) * block_cols
        rhs = jnp.concatenate(
            [
                jnp.concatenate([w[slot_of[at + j]], w[slot_of[at + block_cols + j]]], axis=0)
                for j in range(block_cols)
            ],
            axis=1,
        )
        part = lax.dot_general(
            dy[...], rhs, (((1,), (1,)), ((), ())), preferred_element_type=jnp.float32
        ).astype(keep.dtype)
        keep[:, i * pair : (i + 1) * pair] = part[:half]
        send[:, i * pair : (i + 1) * pair] = part[half:]


def backward(part, slot_of, own, other, w, after):
    block_cols = own.shape[1] // w.shape[1]
    block_rows = slot_of.shape[0] // block_cols
    shape = pltpu.VMEM((own.shape[0], block_rows * w.shape[1] // B_PARTS), own.dtype)
    return pl.pallas_call(
        functools.partial(backward_kernel, part * (block_rows // B_PARTS)),
        out_shape=(shape, shape),
        in_specs=[SMEM, VMEM, VMEM, VMEM] + [ANY] * len(after),
        out_specs=(VMEM, VMEM),
        scratch_shapes=[pltpu.VMEM((2 * own.shape[0], own.shape[1]), own.dtype)],
        compiler_params=PARAMS,
        cost_estimate=pl.CostEstimate(flops=1000, bytes_accessed=1000, transcendentals=0),
    )(slot_of, own, other, resident(w), *after)


def place_forward_kernel(*refs):
    pieces, out = refs[:-1], refs[-1]
    c = lax.axis_index("col")
    width = out.shape[1] // 4
    first_section = lax.axis_index("section") == 0
    for dc in range(4):
        at = (c ^ dc) * width
        for piece in pieces[dc::4]:
            value = jnp.where(first_section, 0.0, piece[...].astype(jnp.float32)).astype(out.dtype)
            out[:, pl.ds(pl.multiple_of(at, 128), piece.shape[1])] = value
            at += piece.shape[1]


def place_forward(pieces):
    rows = pieces[0].shape[0]
    width = sum(piece.shape[1] for piece in pieces)
    return pl.pallas_call(
        place_forward_kernel,
        out_shape=jax.ShapeDtypeStruct((rows, width), pieces[0].dtype),
        in_specs=[VMEM] * len(pieces),
        out_specs=VMEM,
        compiler_params=PARAMS,
    )(*pieces)


def place_backward_kernel(limits, *refs):
    pieces, out = refs[:-1], refs[-1]
    r, c = lax.axis_index("row"), lax.axis_index("col")
    rows = out.shape[0]
    width = out.shape[1] // 2
    for dr in range(2):
        at = (r ^ dr) * width
        for piece in pieces[dr::2]:
            token = (r * 4 + c) * rows + lax.broadcasted_iota(jnp.int32, piece.shape, 0)
            value = jnp.where(token < limits[1], piece[...].astype(jnp.float32), 0.0).astype(out.dtype)
            out[:, pl.ds(pl.multiple_of(at, 128), piece.shape[1])] = value
            at += piece.shape[1]


def place_backward(limits, pieces):
    rows = pieces[0].shape[0]
    width = sum(piece.shape[1] for piece in pieces)
    return pl.pallas_call(
        place_backward_kernel,
        out_shape=jax.ShapeDtypeStruct((rows, width), pieces[0].dtype),
        in_specs=[SMEM] + [VMEM] * len(pieces),
        out_specs=VMEM,
        compiler_params=PARAMS,
    )(limits, *pieces)


def swap(x, axis, by):
    return lax.ppermute(x, axis, [(i, i ^ by) for i in range(lax.axis_size(axis))])


def around(x, axis, by):
    length = lax.axis_size(axis)
    return lax.ppermute(x, axis, [(i, (i + by) % length) for i in range(length)])


def added(a, b):
    return (a.astype(jnp.float32) + b.astype(jnp.float32)).astype(a.dtype)


def grid_2x4(x_fwd, dy_bwd, w_blocks, blk_row, blk_col, blk_count, tok_count, owner_order):
    token_total = x_fwd.shape[0]
    owned = token_total // 8
    slots, size = w_blocks.shape[3], w_blocks.shape[5]
    order = owner_order.reshape(-1)
    limits = tok_count.reshape(2)
    block = token_total // order.shape[0]
    dy_other = swap(dy_bwd, "row", 1)
    w, x, slot_of = prep(
        owned,
        dy_bwd.shape[1] // size,
        blk_count.reshape(1),
        blk_row.reshape(1, slots),
        blk_col.reshape(1, slots),
        owner_order,
        w_blocks.reshape(slots, size, size),
        x_fwd,
    )
    parts = forward(block, order, limits, slot_of, x, w, dy_bwd.shape[1])
    keeps, sends = parts[::2], parts[1::2]
    *sends, dy_other = lax.optimization_barrier((*sends, dy_other))

    y_received = [swap(send, "row", 1) for send in sends]
    y_pieces, dx_pieces = [], []
    forward_sums, backward_sums = [], []
    marks = {}
    for part in range(B_PARTS):
        after = [marks[name] for name in AFTER[part]]
        keep, send = backward(part, slot_of, dy_bwd, dy_other, w, after)
        marks[f"k{part}"] = keep
        if part < F_PARTS:
            summed = added(keeps[part], y_received[part])
            forward_sums.append(summed)
            marks[f'y{part}'] = summed
            shifted = around(summed, "section", 1)
            here, there = shifted[: 2 * owned], swap(shifted[2 * owned :], "col", 2)
            y_pieces += [here[:owned], swap(here[owned:], "col", 1), there[:owned], swap(there[owned:], "col", 1)]
        received = swap(send, "col", 1)
        half = keep.shape[0] // 2
        onward = added(keep[half:], received[half:])
        backward_sums.append(onward)
        marks[f'c{part}'] = onward
        kept = added(keep[:half], received[:half])
        received = swap(onward, "col", 2)
        onward = added(kept[owned:], received[owned:])
        kept = added(kept[:owned], received[:owned])
        dx_pieces += [kept, swap(onward, "row", 1)]
    return place_forward(y_pieces), place_backward(limits, dx_pieces)


def passed_along(shard, axis, by):
    length = lax.axis_size(axis)
    pairs = [(i, i + by) for i in range(length) if 0 <= i + by < length]
    return lax.ppermute(shard, axis, pairs)


def any_grid(x_fwd, dy_bwd, w_blocks, blk_row, blk_col, blk_count, tok_count, owner_order):
    row_count = lax.axis_size("row")
    col_count = lax.axis_size("col")
    token_total, in_width = x_fwd.shape
    out_width = dy_bwd.shape[1]
    slot_total = w_blocks.shape[3]
    block_size = w_blocks.shape[5]
    block_rows = in_width // block_size
    block_cols = out_width // block_size
    owned_rows = token_total // (row_count * col_count)
    weights = w_blocks.reshape(slot_total, block_size, block_size)
    live = (jnp.arange(slot_total) < blk_count.reshape(())).astype(weights.dtype)
    dense_blocks = jnp.zeros((block_rows, block_cols, block_size, block_size), weights.dtype)
    dense_blocks = dense_blocks.at[blk_row.reshape(slot_total), blk_col.reshape(slot_total)].add(
        weights * live[:, None, None]
    )
    dense_weight = jnp.transpose(dense_blocks, (0, 2, 1, 3)).reshape(in_width, out_width)
    limits = tok_count.reshape(2)
    block_total = owner_order.shape[1]
    block_length = token_total // block_total
    token_index = (
        owner_order.reshape(block_total)[:, None] * block_length + jnp.arange(block_length)[None, :]
    ).reshape(token_total)
    ordered_rows = jnp.take(x_fwd, token_index, axis=0)
    ordered_rows = jnp.where(
        (token_index < limits[0])[:, None], ordered_rows, jnp.zeros_like(ordered_rows)
    )
    partial_value = jnp.dot(ordered_rows, dense_weight, preferred_element_type=jnp.float32).astype(
        jnp.bfloat16
    )
    outgoing = partial_value.reshape(row_count * col_count, owned_rows, out_width)
    received = lax.all_to_all(outgoing, ("row", "col"), split_axis=0, concat_axis=2, tiled=True)
    summed = received.reshape(owned_rows, row_count, col_count * out_width).astype(jnp.float32)
    forward_act = jnp.sum(summed, axis=1).astype(jnp.bfloat16)
    y_next = passed_along(forward_act, "section", 1)
    grad_rows = dy_bwd.shape[0]
    grad_index = lax.axis_index("row") * grad_rows + jnp.arange(grad_rows)
    grad_kept = jnp.where((grad_index < limits[1])[:, None], dy_bwd, jnp.zeros_like(dy_bwd))
    grad_partial = lax.dot_general(
        lax.all_gather(grad_kept, "row", axis=0, tiled=True),
        dense_weight,
        (((1,), (1,)), ((), ())),
        preferred_element_type=jnp.float32,
    ).astype(jnp.bfloat16)
    grad_outgoing = grad_partial.reshape(row_count * col_count, owned_rows, in_width)
    grad_received = lax.all_to_all(
        grad_outgoing, ("row", "col"), split_axis=0, concat_axis=2, tiled=True
    )
    grad_summed = grad_received.reshape(owned_rows, row_count, col_count, in_width).astype(
        jnp.float32
    )
    dx_section = (
        jnp.sum(grad_summed, axis=2).reshape(owned_rows, row_count * in_width).astype(jnp.bfloat16)
    )
    return (y_next, dx_section)


def solution(mesh):
    small = mesh.shape["row"] == 2 and mesh.shape["col"] == 4
    return jax.shard_map(
        grid_2x4 if small else any_grid,
        mesh=mesh,
        in_specs=(
            P("section", "row"),
            P(("section", "row"), "col"),
            P("section", "row", "col", None, None, None),
            P("section", "row", "col", None),
            P("section", "row", "col", None),
            P("section", "row", "col"),
            P("section", None),
            P("section", None),
        ),
        out_specs=(P(("section", "row", "col"), None), P(("section", "row", "col"), None)),
        check_vma=False,
    )
```

```python
import functools

import jax
import jax.numpy as jnp
from jax import lax
from jax.experimental import pallas as pl
from jax.experimental.pallas import tpu as pltpu
from jax.sharding import PartitionSpec as P


F_PAIRS = (4, 8)
B_PAIRS = (7, 9, 8)
F_FAR_FIRST = (False, True)
TIES = {
    "b0": ("z0", "x1",),
    "fa0": ("z1",),
    "fb0": ("x0", "b0",),
    "k2": ("c0",),
    "u1": ("d0",),
    "y0": ("d0",),
    "y1": ("d0",),
    "z1": ("z0",),
}

VMEM = pl.BlockSpec(memory_space=pltpu.VMEM)
SMEM = pl.BlockSpec(memory_space=pltpu.SMEM)
ANY = pl.BlockSpec(memory_space=pl.ANY)
HBM = pl.BlockSpec(memory_space=pltpu.HBM)
PARAMS = pltpu.CompilerParams(vmem_limit_bytes=16 * 2**20)


def resident(x):
    return pltpu.with_memory_space_constraint(x, pltpu.VMEM)


def in_hbm(x):
    return pltpu.with_memory_space_constraint(x, pltpu.HBM)


def divisor(n, most):
    return max(d for d in range(1, most + 1) if n % d == 0)


def prep_kernel(
    owned, block_rows, block_cols,
    count, row_hbm, col_hbm, order_hbm, w_hbm, x_hbm,
    w_out, x_out, slot_of,
    row, col, order, w_sem, x_sem, list_sem,
):
    cap = w_hbm.shape[0]
    positions = block_rows * block_cols
    lists = [
        pltpu.make_async_copy(source, target, list_sem.at[i])
        for i, (source, target) in enumerate(
            ((order_hbm, order), (row_hbm, row), (col_hbm, col))
        )
    ]
    for copy in lists:
        copy.start()
    w_copy = pltpu.make_async_copy(w_hbm, w_out.at[pl.ds(0, cap)], w_sem)
    w_copy.start()
    w_out[cap] = jnp.zeros(w_out.shape[1:], w_out.dtype)

    @pl.loop(0, positions // block_cols)
    def _(i):
        for j in range(block_cols):
            slot_of[i * block_cols + j] = cap

    lists[0].wait()
    r, c = lax.axis_index("row"), lax.axis_index("col")
    block = x_hbm.shape[0] // order.shape[1]
    per_owner = owned // block
    copies = []
    at = 0
    for dr in range(2):
        for dc in range(4):
            first = ((r ^ dr) * 4 + (c ^ dc)) * per_owner
            for b in range(per_owner):
                source = pl.multiple_of(order[0, first + b] * block, block)
                copies.append(
                    pltpu.make_async_copy(
                        x_hbm.at[pl.ds(source, block)], x_out.at[pl.ds(at, block)], x_sem.at[len(copies)]
                    )
                )
                copies[-1].start()
                at += block
    for copy in lists[1:]:
        copy.wait()
    live = count[0]
    step = divisor(cap, 20)

    @pl.loop(0, cap // step)
    def _(i):
        for j in range(step):
            k = i * step + j
            place = row[0, k] * block_cols + col[0, k]
            slot_of[jnp.where(k < live, place, positions)] = k

    for copy in copies:
        copy.wait()
    w_copy.wait()


def prep(owned, block_cols, count, row, col, order, weights, x):
    cap, size, _ = weights.shape
    block_rows = x.shape[1] // size
    lists = (row, col, order)
    return pl.pallas_call(
        functools.partial(prep_kernel, owned, block_rows, block_cols),
        out_shape=(
            pltpu.VMEM((cap + 1, size, size), weights.dtype),
            pltpu.VMEM(x.shape, x.dtype),
            jax.ShapeDtypeStruct((block_rows * block_cols + 1,), jnp.int32),
        ),
        in_specs=[SMEM] + [HBM] * 5,
        out_specs=(VMEM, VMEM, SMEM),
        scratch_shapes=[pltpu.SMEM(a.shape, a.dtype) for a in lists]
        + [
            pltpu.SemaphoreType.DMA,
            pltpu.SemaphoreType.DMA((order.shape[1],)),
            pltpu.SemaphoreType.DMA((len(lists),)),
        ],
        compiler_params=PARAMS,
    )(count, *[in_hbm(a) for a in (*lists, weights, x)])


def forward_kernel(block, block_cols, order, limits, slot_of, x, w, *outs):
    r, c = lax.axis_index("row"), lax.axis_index("col")
    rows = x.shape[0]
    half = rows // 2
    per_owner = rows // 8 // block
    size = w.shape[1]
    pair = 2 * size
    tokens = []
    for dr in range(2):
        for dc in range(4):
            for b in range(per_owner):
                first = order[((r ^ dr) * 4 + (c ^ dc)) * per_owner + b] * block
                tokens.append(first + lax.broadcasted_iota(jnp.int32, (block, pair), 0))
    live = jnp.concatenate(tokens, axis=0) < limits[0]
    quarter = half // 2
    column = 0
    for far_first in F_FAR_FIRST:
        if far_first:
            (near, near_send, far), outs = outs[:3], outs[3:]
            places = (
                (near, 0, 0),
                (far, 0, quarter),
                (near_send, 0, half),
                (far, quarter, half + quarter),
            )
        else:
            (keep, send), outs = outs[:2], outs[2:]
            places = ((keep, 0, 0), (keep, quarter, quarter), (send, 0, half), (send, quarter, half + quarter))
        for j in range(places[0][0].shape[1] // pair):
            rhs = jnp.concatenate(
                [
                    jnp.concatenate([w[slot_of[i + column]], w[slot_of[i + column + 1]]], axis=1)
                    for i in range(0, slot_of.shape[0] - 1, block_cols)
                ],
                axis=0,
            )
            part = jnp.dot(x[...], rhs, preferred_element_type=jnp.float32)
            part = jnp.where(live, part, 0.0).astype(x.dtype)
            for out, to, at in places:
                out[to : to + quarter, j * pair : (j + 1) * pair] = part[at : at + quarter]
            column += 2


def forward(block, order, limits, slot_of, x, w, widths):
    half = x.shape[0] // 2
    shapes = []
    for width, far_first in zip(widths, F_FAR_FIRST):
        for rows in (half // 2, half // 2, half) if far_first else (half, half):
            shapes.append(pltpu.VMEM((rows, width), x.dtype))
    return pl.pallas_call(
        functools.partial(forward_kernel, block, sum(widths) // w.shape[1]),
        out_shape=shapes,
        in_specs=[SMEM, SMEM, SMEM, VMEM, VMEM],
        out_specs=[VMEM] * len(shapes),
        compiler_params=PARAMS,
        cost_estimate=pl.CostEstimate(flops=1000, bytes_accessed=1000, transcendentals=0),
    )(order, limits, slot_of, resident(x), resident(w))


def backward_kernel(first, slot_of, own, other, w, *refs):
    keep, send, dy = refs[-3:]
    c = lax.axis_index("col")
    owned = own.shape[0] // 4
    size = w.shape[1]
    block_cols = own.shape[1] // size
    at = 0
    for dk in range(2):
        for dx in range(2):
            rows = pl.ds(pl.multiple_of((c ^ (2 * dx + dk)) * owned, owned), owned)
            for source in (own, other):
                dy[at : at + owned] = source[rows]
                at += owned
    half = keep.shape[0]
    pair = 2 * size
    for i in range(keep.shape[1] // pair):
        at = (first + 2 * i) * block_cols
        rhs = jnp.concatenate(
            [
                jnp.concatenate([w[slot_of[at + j]], w[slot_of[at + block_cols + j]]], axis=0)
                for j in range(block_cols)
            ],
            axis=1,
        )
        part = lax.dot_general(
            dy[...], rhs, (((1,), (1,)), ((), ())), preferred_element_type=jnp.float32
        ).astype(keep.dtype)
        keep[:, i * pair : (i + 1) * pair] = part[:half]
        send[:, i * pair : (i + 1) * pair] = part[half:]


def backward(first, pairs, slot_of, own, other, w, after):
    shape = pltpu.VMEM((own.shape[0], pairs * 2 * w.shape[1]), own.dtype)
    return pl.pallas_call(
        functools.partial(backward_kernel, 2 * first),
        out_shape=(shape, shape),
        in_specs=[SMEM, VMEM, VMEM, VMEM] + [ANY] * len(after),
        out_specs=(VMEM, VMEM),
        scratch_shapes=[pltpu.VMEM((2 * own.shape[0], own.shape[1]), own.dtype)],
        compiler_params=PARAMS,
        cost_estimate=pl.CostEstimate(flops=1000, bytes_accessed=1000, transcendentals=0),
    )(slot_of, own, other, resident(w), *after)


def place_forward_kernel(*refs):
    pieces, out = refs[:-1], refs[-1]
    c = lax.axis_index("col")
    width = out.shape[1] // 4
    first_section = lax.axis_index("section") == 0
    for dc in range(4):
        at = (c ^ dc) * width
        for piece in pieces[dc::4]:
            value = jnp.where(first_section, 0.0, piece[...].astype(jnp.float32)).astype(out.dtype)
            out[:, pl.ds(pl.multiple_of(at, 128), piece.shape[1])] = value
            at += piece.shape[1]


def place_forward(pieces):
    rows = pieces[0].shape[0]
    width = sum(piece.shape[1] for piece in pieces)
    return pl.pallas_call(
        place_forward_kernel,
        out_shape=jax.ShapeDtypeStruct((rows, width), pieces[0].dtype),
        in_specs=[VMEM] * len(pieces),
        out_specs=VMEM,
        compiler_params=PARAMS,
    )(*pieces)


def place_backward_kernel(limits, *refs):
    pieces, out = refs[:-1], refs[-1]
    r, c = lax.axis_index("row"), lax.axis_index("col")
    rows = out.shape[0]
    width = out.shape[1] // 2
    for dr in range(2):
        at = (r ^ dr) * width
        for piece in pieces[dr::2]:
            token = (r * 4 + c) * rows + lax.broadcasted_iota(jnp.int32, piece.shape, 0)
            value = jnp.where(token < limits[1], piece[...].astype(jnp.float32), 0.0).astype(out.dtype)
            out[:, pl.ds(pl.multiple_of(at, 128), piece.shape[1])] = value
            at += piece.shape[1]


def place_backward(limits, pieces):
    rows = pieces[0].shape[0]
    width = sum(piece.shape[1] for piece in pieces)
    return pl.pallas_call(
        place_backward_kernel,
        out_shape=jax.ShapeDtypeStruct((rows, width), pieces[0].dtype),
        in_specs=[SMEM] + [VMEM] * len(pieces),
        out_specs=VMEM,
        compiler_params=PARAMS,
    )(limits, *pieces)


def swap(x, axis, by):
    return lax.ppermute(x, axis, [(i, i ^ by) for i in range(lax.axis_size(axis))])


def around(x, axis, by):
    length = lax.axis_size(axis)
    return lax.ppermute(x, axis, [(i, (i + by) % length) for i in range(length)])


def tied(x, *others):
    return lax.optimization_barrier((x, *others))[0]


def added(a, b):
    return (a.astype(jnp.float32) + b.astype(jnp.float32)).astype(a.dtype)


def grid_2x4(x_fwd, dy_bwd, w_blocks, blk_row, blk_col, blk_count, tok_count, owner_order):
    token_total = x_fwd.shape[0]
    owned = token_total // 8
    slots, size = w_blocks.shape[3], w_blocks.shape[5]
    order = owner_order.reshape(-1)
    limits = tok_count.reshape(2)
    block = token_total // order.shape[0]
    w, x, slot_of = prep(
        owned,
        dy_bwd.shape[1] // size,
        blk_count.reshape(1),
        blk_row.reshape(1, slots),
        blk_col.reshape(1, slots),
        owner_order,
        w_blocks.reshape(slots, size, size),
        x_fwd,
    )
    widths = [size * 2 * share for share in F_PAIRS]
    parts = forward(block, order, limits, slot_of, x, w, widths)
    grouped = []
    for far_first in F_FAR_FIRST:
        count = 3 if far_first else 2
        grouped.append(parts[:count])
        parts = parts[count:]
    half, quarter = dy_bwd.shape[0], dy_bwd.shape[0] // 2
    made = {}

    def get(name):
        if name not in made:
            made[name] = make(name)
        return made[name]

    def make(name):
        kind, at = name[:-1], int(name[-1])
        after = [get(other)[0] for other in TIES.get(name, ())]
        if kind == "d":
            return (swap(dy_bwd, "row", 1),)
        if kind == "y":
            return (added(grouped[at][0], swap(tied(grouped[at][1], *after), "row", 1)),)
        if kind == "u":
            return (swap(tied(grouped[at][2], *after), "col", 2),)
        if kind == "v":
            far = get(f"u{at}")[0]
            return (added(far[:quarter], swap(tied(far[quarter:], *after), "row", 1)),)
        if kind == "z":
            total = get(f"y{at}")[0]
            if F_FAR_FIRST[at]:
                far = get(f"v{at}")[0]
                total = jnp.concatenate([total[:owned], far[:owned], total[owned:], far[owned:]])
            return (around(tied(total, *after), "section", 1),)
        if kind == "fx":
            return (swap(tied(get(f"z{at}")[0][quarter:], *after), "col", 2),)
        if kind == "fa":
            if F_FAR_FIRST[at]:
                return (swap(tied(get(f"z{at}")[0][quarter:], *after), "col", 1),)
            return (swap(tied(get(f"z{at}")[0][owned:quarter], *after), "col", 1),)
        if kind == "fb":
            return (swap(tied(get(f"fx{at}")[0][owned:], *after), "col", 1),)
        if kind == "k":
            return backward(sum(B_PAIRS[:at]), B_PAIRS[at], slot_of, dy_bwd, get("d0")[0], w, after)
        if kind == "c":
            keep, send = get(f"k{at}")
            received = swap(tied(send, *after), "col", 1)
            return added(keep[quarter:], received[quarter:]), added(keep[:quarter], received[:quarter])
        if kind == "x":
            onward, kept = get(f"c{at}")
            received = swap(tied(onward, *after), "col", 2)
            return added(kept[owned:], received[owned:]), added(kept[:owned], received[:owned])
        if kind == "b":
            return (swap(tied(get(f"x{at}")[0], *after), "row", 1),)

    y_pieces, dx_pieces = [], []
    for at in range(len(F_PAIRS)):
        here, beside = get(f"z{at}")[0], get(f"fa{at}")[0]
        if F_FAR_FIRST[at]:
            y_pieces += [here[:owned], beside[:owned], here[owned:quarter], beside[owned:]]
        else:
            y_pieces += [here[:owned], beside, get(f"fx{at}")[0][:owned], get(f"fb{at}")[0]]
    for at in range(len(B_PAIRS)):
        dx_pieces += [get(f"x{at}")[1], get(f"b{at}")[0]]
    return place_forward(y_pieces), place_backward(limits, dx_pieces)


def passed_along(shard, axis, by):
    length = lax.axis_size(axis)
    pairs = [(i, i + by) for i in range(length) if 0 <= i + by < length]
    return lax.ppermute(shard, axis, pairs)


def any_grid(x_fwd, dy_bwd, w_blocks, blk_row, blk_col, blk_count, tok_count, owner_order):
    row_count = lax.axis_size("row")
    col_count = lax.axis_size("col")
    token_total, in_width = x_fwd.shape
    out_width = dy_bwd.shape[1]
    slot_total = w_blocks.shape[3]
    block_size = w_blocks.shape[5]
    block_rows = in_width // block_size
    block_cols = out_width // block_size
    owned_rows = token_total // (row_count * col_count)
    weights = w_blocks.reshape(slot_total, block_size, block_size)
    live = (jnp.arange(slot_total) < blk_count.reshape(())).astype(weights.dtype)
    dense_blocks = jnp.zeros((block_rows, block_cols, block_size, block_size), weights.dtype)
    dense_blocks = dense_blocks.at[blk_row.reshape(slot_total), blk_col.reshape(slot_total)].add(
        weights * live[:, None, None]
    )
    dense_weight = jnp.transpose(dense_blocks, (0, 2, 1, 3)).reshape(in_width, out_width)
    limits = tok_count.reshape(2)
    block_total = owner_order.shape[1]
    block_length = token_total // block_total
    token_index = (
        owner_order.reshape(block_total)[:, None] * block_length + jnp.arange(block_length)[None, :]
    ).reshape(token_total)
    ordered_rows = jnp.take(x_fwd, token_index, axis=0)
    ordered_rows = jnp.where(
        (token_index < limits[0])[:, None], ordered_rows, jnp.zeros_like(ordered_rows)
    )
    partial_value = jnp.dot(ordered_rows, dense_weight, preferred_element_type=jnp.float32).astype(
        jnp.bfloat16
    )
    outgoing = partial_value.reshape(row_count * col_count, owned_rows, out_width)
    received = lax.all_to_all(outgoing, ("row", "col"), split_axis=0, concat_axis=2, tiled=True)
    summed = received.reshape(owned_rows, row_count, col_count * out_width).astype(jnp.float32)
    forward_act = jnp.sum(summed, axis=1).astype(jnp.bfloat16)
    y_next = passed_along(forward_act, "section", 1)
    grad_rows = dy_bwd.shape[0]
    grad_index = lax.axis_index("row") * grad_rows + jnp.arange(grad_rows)
    grad_kept = jnp.where((grad_index < limits[1])[:, None], dy_bwd, jnp.zeros_like(dy_bwd))
    grad_partial = lax.dot_general(
        lax.all_gather(grad_kept, "row", axis=0, tiled=True),
        dense_weight,
        (((1,), (1,)), ((), ())),
        preferred_element_type=jnp.float32,
    ).astype(jnp.bfloat16)
    grad_outgoing = grad_partial.reshape(row_count * col_count, owned_rows, in_width)
    grad_received = lax.all_to_all(
        grad_outgoing, ("row", "col"), split_axis=0, concat_axis=2, tiled=True
    )
    grad_summed = grad_received.reshape(owned_rows, row_count, col_count, in_width).astype(
        jnp.float32
    )
    dx_section = (
        jnp.sum(grad_summed, axis=2).reshape(owned_rows, row_count * in_width).astype(jnp.bfloat16)
    )
    return (y_next, dx_section)


def solution(mesh):
    small = mesh.shape["row"] == 2 and mesh.shape["col"] == 4
    return jax.shard_map(
        grid_2x4 if small else any_grid,
        mesh=mesh,
        in_specs=(
            P("section", "row"),
            P(("section", "row"), "col"),
            P("section", "row", "col", None, None, None),
            P("section", "row", "col", None),
            P("section", "row", "col", None),
            P("section", "row", "col"),
            P("section", None),
            P("section", None),
        ),
        out_specs=(P(("section", "row", "col"), None), P(("section", "row", "col"), None)),
        check_vma=False,
    )
```

```python
import functools

import jax
import jax.numpy as jnp
from jax import lax
from jax.experimental import pallas as pl
from jax.experimental.pallas import tpu as pltpu
from jax.sharding import PartitionSpec as P


F_PAIRS = (6, 6)
B_PAIRS = (8, 9, 7)
JOINT = 1
F_FAR_FIRST = (0, 1)
TRACE_FIRST = ()
B_JOINED = 1
C_SPLIT = 1
TIES = {
    "b0": ("x1", "z1",),
    "k2": ("c0",),
    "u1": ("d0",),
    "x1": ("y0",),
    "y0": ("d0",),
    "y1": ("c0",),
}

VMEM = pl.BlockSpec(memory_space=pltpu.VMEM)
SMEM = pl.BlockSpec(memory_space=pltpu.SMEM)
ANY = pl.BlockSpec(memory_space=pl.ANY)
HBM = pl.BlockSpec(memory_space=pltpu.HBM)
PARAMS = pltpu.CompilerParams(vmem_limit_bytes=16 * 2**20)


def resident(x):
    return pltpu.with_memory_space_constraint(x, pltpu.VMEM)


def in_hbm(x):
    return pltpu.with_memory_space_constraint(x, pltpu.HBM)


def divisor(n, most):
    return max(d for d in range(1, most + 1) if n % d == 0)


def prep_kernel(
    owned, block_rows, block_cols,
    count, row_hbm, col_hbm, order_hbm, w_hbm, x_hbm,
    w_out, x_out, slot_of,
    row, col, order, w_sem, x_sem, list_sem,
):
    cap = w_hbm.shape[0]
    positions = block_rows * block_cols
    lists = [
        pltpu.make_async_copy(source, target, list_sem.at[i])
        for i, (source, target) in enumerate(
            ((order_hbm, order), (row_hbm, row), (col_hbm, col))
        )
    ]
    for copy in lists:
        copy.start()
    w_copy = pltpu.make_async_copy(w_hbm, w_out.at[pl.ds(0, cap)], w_sem)
    w_copy.start()
    w_out[cap] = jnp.zeros(w_out.shape[1:], w_out.dtype)

    @pl.loop(0, positions // block_cols)
    def _(i):
        for j in range(block_cols):
            slot_of[i * block_cols + j] = cap

    lists[0].wait()
    r, c = lax.axis_index("row"), lax.axis_index("col")
    block = x_hbm.shape[0] // order.shape[1]
    per_owner = owned // block
    copies = []
    at = 0
    for dr in range(2):
        for dc in range(4):
            first = ((r ^ dr) * 4 + (c ^ dc)) * per_owner
            for b in range(per_owner):
                source = pl.multiple_of(order[0, first + b] * block, block)
                copies.append(
                    pltpu.make_async_copy(
                        x_hbm.at[pl.ds(source, block)], x_out.at[pl.ds(at, block)], x_sem.at[len(copies)]
                    )
                )
                copies[-1].start()
                at += block
    for copy in lists[1:]:
        copy.wait()
    live = count[0]
    step = divisor(cap, 20)

    @pl.loop(0, cap // step)
    def _(i):
        for j in range(step):
            k = i * step + j
            place = row[0, k] * block_cols + col[0, k]
            slot_of[jnp.where(k < live, place, positions)] = k

    for copy in copies:
        copy.wait()
    w_copy.wait()


def prep(owned, block_cols, count, row, col, order, weights, x):
    cap, size, _ = weights.shape
    block_rows = x.shape[1] // size
    lists = (row, col, order)
    return pl.pallas_call(
        functools.partial(prep_kernel, owned, block_rows, block_cols),
        out_shape=(
            pltpu.VMEM((cap + 1, size, size), weights.dtype),
            pltpu.VMEM(x.shape, x.dtype),
            jax.ShapeDtypeStruct((block_rows * block_cols + 1,), jnp.int32),
        ),
        in_specs=[SMEM] + [HBM] * 5,
        out_specs=(VMEM, VMEM, SMEM),
        scratch_shapes=[pltpu.SMEM(a.shape, a.dtype) for a in lists]
        + [
            pltpu.SemaphoreType.DMA,
            pltpu.SemaphoreType.DMA((order.shape[1],)),
            pltpu.SemaphoreType.DMA((len(lists),)),
        ],
        compiler_params=PARAMS,
    )(count, *[in_hbm(a) for a in (*lists, weights, x)])


def forward_kernel(block, block_cols, order, limits, slot_of, x, w, *outs):
    r, c = lax.axis_index("row"), lax.axis_index("col")
    rows = x.shape[0]
    half = rows // 2
    per_owner = rows // 8 // block
    size = w.shape[1]
    pair = 2 * size
    tokens = []
    for dr in range(2):
        for dc in range(4):
            for b in range(per_owner):
                first = order[((r ^ dr) * 4 + (c ^ dc)) * per_owner + b] * block
                tokens.append(first + lax.broadcasted_iota(jnp.int32, (block, pair), 0))
    live = jnp.concatenate(tokens, axis=0) < limits[0]
    quarter = half // 2
    column = 0
    for far_first in F_FAR_FIRST:
        if far_first:
            (near, near_send, far), outs = outs[:3], outs[3:]
            places = (
                (near, 0, 0),
                (far, 0, quarter),
                (near_send, 0, half),
                (far, quarter, half + quarter),
            )
        else:
            (keep, send), outs = outs[:2], outs[2:]
            places = ((keep, 0, 0), (keep, quarter, quarter), (send, 0, half), (send, quarter, half + quarter))
        for j in range(places[0][0].shape[1] // pair):
            rhs = jnp.concatenate(
                [
                    jnp.concatenate([w[slot_of[i + column]], w[slot_of[i + column + 1]]], axis=1)
                    for i in range(0, slot_of.shape[0] - 1, block_cols)
                ],
                axis=0,
            )
            part = jnp.dot(x[...], rhs, preferred_element_type=jnp.float32)
            part = jnp.where(live, part, 0.0).astype(x.dtype)
            for out, to, at in places:
                out[to : to + quarter, j * pair : (j + 1) * pair] = part[at : at + quarter]
            column += 2


def forward(block, order, limits, slot_of, x, w, widths):
    half = x.shape[0] // 2
    shapes = []
    for width, far_first in zip(widths, F_FAR_FIRST):
        for rows in (half // 2, half // 2, half) if far_first else (half, half):
            shapes.append(pltpu.VMEM((rows, width), x.dtype))
    return pl.pallas_call(
        functools.partial(forward_kernel, block, sum(widths) // w.shape[1]),
        out_shape=shapes,
        in_specs=[SMEM, SMEM, SMEM, VMEM, VMEM],
        out_specs=[VMEM] * len(shapes),
        compiler_params=PARAMS,
        cost_estimate=pl.CostEstimate(flops=1000, bytes_accessed=1000, transcendentals=0),
    )(order, limits, slot_of, resident(x), resident(w))


def backward_kernel(first, slot_of, own, other, w, *refs):
    keep, send, dy = refs[-3:]
    c = lax.axis_index("col")
    owned = own.shape[0] // 4
    size = w.shape[1]
    block_cols = own.shape[1] // size
    at = 0
    for dk in range(2):
        for dx in range(2):
            rows = pl.ds(pl.multiple_of((c ^ (2 * dx + dk)) * owned, owned), owned)
            for source in (own, other):
                dy[at : at + owned] = source[rows]
                at += owned
    half = keep.shape[0]
    pair = 2 * size
    for i in range(keep.shape[1] // pair):
        at = (first + 2 * i) * block_cols
        rhs = jnp.concatenate(
            [
                jnp.concatenate([w[slot_of[at + j]], w[slot_of[at + block_cols + j]]], axis=0)
                for j in range(block_cols)
            ],
            axis=1,
        )
        part = lax.dot_general(
            dy[...], rhs, (((1,), (1,)), ((), ())), preferred_element_type=jnp.float32
        ).astype(keep.dtype)
        keep[:, i * pair : (i + 1) * pair] = part[:half]
        send[:, i * pair : (i + 1) * pair] = part[half:]


def backward(first, pairs, slot_of, own, other, w, after):
    shape = pltpu.VMEM((own.shape[0], pairs * 2 * w.shape[1]), own.dtype)
    return pl.pallas_call(
        functools.partial(backward_kernel, 2 * first),
        out_shape=(shape, shape),
        in_specs=[SMEM, VMEM, VMEM, VMEM] + [ANY] * len(after),
        out_specs=(VMEM, VMEM),
        scratch_shapes=[pltpu.VMEM((2 * own.shape[0], own.shape[1]), own.dtype)],
        compiler_params=PARAMS,
        cost_estimate=pl.CostEstimate(flops=1000, bytes_accessed=1000, transcendentals=0),
    )(slot_of, own, other, resident(w), *after)


def place_kernel(counts, limits, *refs):
    y_out, dx_out = refs[-2:]
    lists = []
    for count in counts:
        lists.append(refs[:count])
        refs = refs[count:]
    r, c = lax.axis_index("row"), lax.axis_index("col")
    rows = y_out.shape[0]
    first_section = lax.axis_index("section") == 0
    for dr, pieces in enumerate(lists[:2]):
        at = (r ^ dr) * (dx_out.shape[1] // 2)
        for piece in pieces:
            token = (r * 4 + c) * rows + lax.broadcasted_iota(jnp.int32, piece.shape, 0)
            value = jnp.where(token < limits[1], piece[...].astype(jnp.float32), 0.0)
            dx_out[:, pl.ds(pl.multiple_of(at, 128), piece.shape[1])] = value.astype(dx_out.dtype)
            at += piece.shape[1]
    width = y_out.shape[1] // 4
    for dc, pieces in zip((0, 2, 1, 3), lists[2:4] + [lists[4], lists[4]]):
        at = (c ^ dc) * width
        for piece in pieces:
            value = piece[...] if dc % 2 == 0 else piece[:, dc // 2 * width : (dc // 2 + 1) * width]
            value = jnp.where(first_section, 0.0, value.astype(jnp.float32)).astype(y_out.dtype)
            y_out[:, pl.ds(pl.multiple_of(at, 128), value.shape[1])] = value
            at += value.shape[1]


def place(limits, width, lists):
    pieces = [piece for each in lists for piece in each]
    shape = jax.ShapeDtypeStruct((pieces[0].shape[0], width), pieces[0].dtype)
    return pl.pallas_call(
        functools.partial(place_kernel, [len(each) for each in lists]),
        out_shape=[shape] * 2,
        in_specs=[SMEM] + [VMEM] * len(pieces),
        out_specs=[VMEM] * 2,
        compiler_params=PARAMS,
    )(limits, *pieces)


def swap(x, axis, by):
    return lax.ppermute(x, axis, [(i, i ^ by) for i in range(lax.axis_size(axis))])


def around(x, axis, by):
    length = lax.axis_size(axis)
    return lax.ppermute(x, axis, [(i, (i + by) % length) for i in range(length)])


def tied(x, *others):
    return lax.optimization_barrier((x, *others))[0]


def added(a, b):
    return (a.astype(jnp.float32) + b.astype(jnp.float32)).astype(a.dtype)


def grid_2x4(x_fwd, dy_bwd, w_blocks, blk_row, blk_col, blk_count, tok_count, owner_order):
    token_total = x_fwd.shape[0]
    owned = token_total // 8
    slots, size = w_blocks.shape[3], w_blocks.shape[5]
    order = owner_order.reshape(-1)
    limits = tok_count.reshape(2)
    block = token_total // order.shape[0]
    w, x, slot_of = prep(
        owned,
        dy_bwd.shape[1] // size,
        blk_count.reshape(1),
        blk_row.reshape(1, slots),
        blk_col.reshape(1, slots),
        owner_order,
        w_blocks.reshape(slots, size, size),
        x_fwd,
    )
    widths = [size * 2 * share for share in F_PAIRS]
    parts = forward(block, order, limits, slot_of, x, w, widths)
    grouped = []
    for far_first in F_FAR_FIRST:
        count = 3 if far_first else 2
        grouped.append(parts[:count])
        parts = parts[count:]
    half, quarter = dy_bwd.shape[0], dy_bwd.shape[0] // 2
    made = {}

    def get(name):
        if name not in made:
            made[name] = make(name)
        return made[name]

    def make(name):
        kind, at = name[:-1], int(name[-1])
        after = [get(other)[0] for other in TIES.get(name, ())]
        if kind == "d":
            return (swap(dy_bwd, "row", 1),)
        if kind == "y":
            return (added(grouped[at][0], swap(tied(grouped[at][1], *after), "row", 1)),)
        if kind == "u":
            return (swap(tied(grouped[at][2], *after), "col", 2),)
        if kind == "v":
            far = get(f"u{at}")[0]
            return (added(far[:quarter], swap(tied(far[quarter:], *after), "row", 1)),)
        if kind == "z":
            total = get(f"y{at}")[0]
            if F_FAR_FIRST[at] == JOINT:
                far = get(f"v{at}")[0]
                total = jnp.concatenate([total[:owned], far[:owned], total[owned:], far[owned:]])
            return (around(tied(total, *after), "section", 1),)
        if kind == "w":
            return (around(tied(get(f"v{at}")[0], *after), "section", 1),)
        if kind == "fx":
            return (swap(tied(get(f"z{at}")[0][quarter:], *after), "col", 2),)
        if kind == "fc":
            near, beyond = [], []
            for part, far_first in enumerate(F_FAR_FIRST):
                here = get(f"z{part}")[0]
                if far_first == JOINT:
                    near.append(here[quarter : quarter + owned])
                    beyond.append(here[quarter + owned :])
                else:
                    near.append(here[owned:quarter])
                    beyond.append(get(f"w{part}" if far_first else f"fx{part}")[0][owned:])
            return (swap(tied(jnp.concatenate(near + beyond, axis=1), *after), "col", 1),)
        if kind == "k":
            return backward(sum(B_PAIRS[:at]), B_PAIRS[at], slot_of, dy_bwd, get("d0")[0], w, after)
        if kind == "c":
            keep, send = get(f"k{at}")
            send = tied(send, *after)
            step = send.shape[0] // C_SPLIT
            received = jnp.concatenate(
                [swap(send[i * step : (i + 1) * step], "col", 1) for i in range(C_SPLIT)]
            )
            return added(keep[quarter:], received[quarter:]), added(keep[:quarter], received[:quarter])
        if kind == "x":
            onward, kept = get(f"c{at}")
            received = swap(tied(onward, *after), "col", 2)
            return added(kept[owned:], received[owned:]), added(kept[:owned], received[:owned])
        if kind == "b":
            onward = [get(f"x{part}")[0] for part in (range(B_JOINED) if at < B_JOINED else (at,))]
            return (swap(tied(jnp.concatenate(onward, axis=1), *after), "row", 1),)

    for name in TRACE_FIRST:
        get(name)
    own, beyond = [], []
    for part, far_first in enumerate(F_FAR_FIRST):
        here = get(f"z{part}")[0]
        own.append(here[:owned])
        if far_first == JOINT:
            beyond.append(here[owned:quarter])
        else:
            beyond.append(get(f"w{part}" if far_first else f"fx{part}")[0][:owned])
    parts = range(len(B_PAIRS))
    kept = [get(f"x{part}")[1] for part in parts]
    received = [get(f"b{part}")[0] for part in parts if part == 0 or part >= B_JOINED]
    y_next, dx_section = place(limits, 4 * dy_bwd.shape[1], [kept, received, own, beyond, [get("fc0")[0]]])
    return y_next, dx_section


def passed_along(shard, axis, by):
    length = lax.axis_size(axis)
    pairs = [(i, i + by) for i in range(length) if 0 <= i + by < length]
    return lax.ppermute(shard, axis, pairs)


def any_grid(x_fwd, dy_bwd, w_blocks, blk_row, blk_col, blk_count, tok_count, owner_order):
    row_count = lax.axis_size("row")
    col_count = lax.axis_size("col")
    token_total, in_width = x_fwd.shape
    out_width = dy_bwd.shape[1]
    slot_total = w_blocks.shape[3]
    block_size = w_blocks.shape[5]
    block_rows = in_width // block_size
    block_cols = out_width // block_size
    owned_rows = token_total // (row_count * col_count)
    weights = w_blocks.reshape(slot_total, block_size, block_size)
    live = (jnp.arange(slot_total) < blk_count.reshape(())).astype(weights.dtype)
    dense_blocks = jnp.zeros((block_rows, block_cols, block_size, block_size), weights.dtype)
    dense_blocks = dense_blocks.at[blk_row.reshape(slot_total), blk_col.reshape(slot_total)].add(
        weights * live[:, None, None]
    )
    dense_weight = jnp.transpose(dense_blocks, (0, 2, 1, 3)).reshape(in_width, out_width)
    limits = tok_count.reshape(2)
    block_total = owner_order.shape[1]
    block_length = token_total // block_total
    token_index = (
        owner_order.reshape(block_total)[:, None] * block_length + jnp.arange(block_length)[None, :]
    ).reshape(token_total)
    ordered_rows = jnp.take(x_fwd, token_index, axis=0)
    ordered_rows = jnp.where(
        (token_index < limits[0])[:, None], ordered_rows, jnp.zeros_like(ordered_rows)
    )
    partial_value = jnp.dot(ordered_rows, dense_weight, preferred_element_type=jnp.float32).astype(
        jnp.bfloat16
    )
    outgoing = partial_value.reshape(row_count * col_count, owned_rows, out_width)
    received = lax.all_to_all(outgoing, ("row", "col"), split_axis=0, concat_axis=2, tiled=True)
    summed = received.reshape(owned_rows, row_count, col_count * out_width).astype(jnp.float32)
    forward_act = jnp.sum(summed, axis=1).astype(jnp.bfloat16)
    y_next = passed_along(forward_act, "section", 1)
    grad_rows = dy_bwd.shape[0]
    grad_index = lax.axis_index("row") * grad_rows + jnp.arange(grad_rows)
    grad_kept = jnp.where((grad_index < limits[1])[:, None], dy_bwd, jnp.zeros_like(dy_bwd))
    grad_partial = lax.dot_general(
        lax.all_gather(grad_kept, "row", axis=0, tiled=True),
        dense_weight,
        (((1,), (1,)), ((), ())),
        preferred_element_type=jnp.float32,
    ).astype(jnp.bfloat16)
    grad_outgoing = grad_partial.reshape(row_count * col_count, owned_rows, in_width)
    grad_received = lax.all_to_all(
        grad_outgoing, ("row", "col"), split_axis=0, concat_axis=2, tiled=True
    )
    grad_summed = grad_received.reshape(owned_rows, row_count, col_count, in_width).astype(
        jnp.float32
    )
    dx_section = (
        jnp.sum(grad_summed, axis=2).reshape(owned_rows, row_count * in_width).astype(jnp.bfloat16)
    )
    return (y_next, dx_section)


def solution(mesh):
    small = mesh.shape["row"] == 2 and mesh.shape["col"] == 4
    return jax.shard_map(
        grid_2x4 if small else any_grid,
        mesh=mesh,
        in_specs=(
            P("section", "row"),
            P(("section", "row"), "col"),
            P("section", "row", "col", None, None, None),
            P("section", "row", "col", None),
            P("section", "row", "col", None),
            P("section", "row", "col"),
            P("section", None),
            P("section", None),
        ),
        out_specs=(P(("section", "row", "col"), None), P(("section", "row", "col"), None)),
        check_vma=False,
    )
```

```python
import functools

import jax
import jax.numpy as jnp
from jax import lax
from jax.experimental import pallas as pl
from jax.experimental.pallas import tpu as pltpu
from jax.sharding import PartitionSpec as P


F_PAIRS = (6, 6)
B_PAIRS = (8, 10, 6)
JOINT = 1
F_FAR_FIRST = (0, 1)
TRACE_FIRST = ()
B_JOINED = 1
C_SPLIT = 1
TIES = {
    "k2": ("c0",),
    "u1": ("d0",),
    "x1": ("y0",),
    "y0": ("d0",),
    "y1": ("c0",),
}

VMEM = pl.BlockSpec(memory_space=pltpu.VMEM)
SMEM = pl.BlockSpec(memory_space=pltpu.SMEM)
ANY = pl.BlockSpec(memory_space=pl.ANY)
HBM = pl.BlockSpec(memory_space=pltpu.HBM)
PARAMS = pltpu.CompilerParams(vmem_limit_bytes=16 * 2**20)


def resident(x):
    return pltpu.with_memory_space_constraint(x, pltpu.VMEM)


def in_hbm(x):
    return pltpu.with_memory_space_constraint(x, pltpu.HBM)


def divisor(n, most):
    return max(d for d in range(1, most + 1) if n % d == 0)


def prep_kernel(
    owned, block_rows, block_cols,
    count, row_hbm, col_hbm, order_hbm, w_hbm, x_hbm,
    w_out, x_out, slot_of,
    row, col, order, w_sem, x_sem, list_sem,
):
    cap = w_hbm.shape[0]
    positions = block_rows * block_cols
    lists = [
        pltpu.make_async_copy(source, target, list_sem.at[i])
        for i, (source, target) in enumerate(
            ((order_hbm, order), (row_hbm, row), (col_hbm, col))
        )
    ]
    for copy in lists:
        copy.start()
    w_copy = pltpu.make_async_copy(w_hbm, w_out.at[pl.ds(0, cap)], w_sem)
    w_copy.start()
    w_out[cap] = jnp.zeros(w_out.shape[1:], w_out.dtype)

    @pl.loop(0, positions // block_cols)
    def _(i):
        for j in range(block_cols):
            slot_of[i * block_cols + j] = cap

    lists[0].wait()
    r, c = lax.axis_index("row"), lax.axis_index("col")
    block = x_hbm.shape[0] // order.shape[1]
    per_owner = owned // block
    copies = []
    at = 0
    for dr in range(2):
        for dc in range(4):
            first = ((r ^ dr) * 4 + (c ^ dc)) * per_owner
            for b in range(per_owner):
                source = pl.multiple_of(order[0, first + b] * block, block)
                copies.append(
                    pltpu.make_async_copy(
                        x_hbm.at[pl.ds(source, block)], x_out.at[pl.ds(at, block)], x_sem.at[len(copies)]
                    )
                )
                copies[-1].start()
                at += block
    for copy in lists[1:]:
        copy.wait()
    live = count[0]
    step = divisor(cap, 20)

    @pl.loop(0, cap // step)
    def _(i):
        for j in range(step):
            k = i * step + j
            place = row[0, k] * block_cols + col[0, k]
            slot_of[jnp.where(k < live, place, positions)] = k

    for copy in copies:
        copy.wait()
    w_copy.wait()


def prep(owned, block_cols, count, row, col, order, weights, x):
    cap, size, _ = weights.shape
    block_rows = x.shape[1] // size
    lists = (row, col, order)
    return pl.pallas_call(
        functools.partial(prep_kernel, owned, block_rows, block_cols),
        out_shape=(
            pltpu.VMEM((cap + 1, size, size), weights.dtype),
            pltpu.VMEM(x.shape, x.dtype),
            jax.ShapeDtypeStruct((block_rows * block_cols + 1,), jnp.int32),
        ),
        in_specs=[SMEM] + [HBM] * 5,
        out_specs=(VMEM, VMEM, SMEM),
        scratch_shapes=[pltpu.SMEM(a.shape, a.dtype) for a in lists]
        + [
            pltpu.SemaphoreType.DMA,
            pltpu.SemaphoreType.DMA((order.shape[1],)),
            pltpu.SemaphoreType.DMA((len(lists),)),
        ],
        compiler_params=PARAMS,
    )(count, *[in_hbm(a) for a in (*lists, weights, x)])


def forward_kernel(block, block_cols, order, limits, slot_of, x, w, *outs):
    r, c = lax.axis_index("row"), lax.axis_index("col")
    rows = x.shape[0]
    half = rows // 2
    per_owner = rows // 8 // block
    size = w.shape[1]
    pair = 2 * size
    tokens = []
    for dr in range(2):
        for dc in range(4):
            for b in range(per_owner):
                first = order[((r ^ dr) * 4 + (c ^ dc)) * per_owner + b] * block
                tokens.append(first + lax.broadcasted_iota(jnp.int32, (block, pair), 0))
    live = jnp.concatenate(tokens, axis=0) < limits[0]
    quarter = half // 2
    column = 0
    for far_first in F_FAR_FIRST:
        if far_first:
            (near, near_send, far), outs = outs[:3], outs[3:]
            places = (
                (near, 0, 0),
                (far, 0, quarter),
                (near_send, 0, half),
                (far, quarter, half + quarter),
            )
        else:
            (keep, send), outs = outs[:2], outs[2:]
            places = ((keep, 0, 0), (keep, quarter, quarter), (send, 0, half), (send, quarter, half + quarter))
        for j in range(places[0][0].shape[1] // pair):
            rhs = jnp.concatenate(
                [
                    jnp.concatenate([w[slot_of[i + column]], w[slot_of[i + column + 1]]], axis=1)
                    for i in range(0, slot_of.shape[0] - 1, block_cols)
                ],
                axis=0,
            )
            part = jnp.dot(x[...], rhs, preferred_element_type=jnp.float32)
            part = jnp.where(live, part, 0.0).astype(x.dtype)
            for out, to, at in places:
                out[to : to + quarter, j * pair : (j + 1) * pair] = part[at : at + quarter]
            column += 2


def forward(block, order, limits, slot_of, x, w, widths):
    half = x.shape[0] // 2
    shapes = []
    for width, far_first in zip(widths, F_FAR_FIRST):
        for rows in (half // 2, half // 2, half) if far_first else (half, half):
            shapes.append(pltpu.VMEM((rows, width), x.dtype))
    return pl.pallas_call(
        functools.partial(forward_kernel, block, sum(widths) // w.shape[1]),
        out_shape=shapes,
        in_specs=[SMEM, SMEM, SMEM, VMEM, VMEM],
        out_specs=[VMEM] * len(shapes),
        compiler_params=PARAMS,
        cost_estimate=pl.CostEstimate(flops=1000, bytes_accessed=1000, transcendentals=0),
    )(order, limits, slot_of, resident(x), resident(w))


def backward_kernel(first, slot_of, own, other, w, *refs):
    keep, send, dy = refs[-3:]
    c = lax.axis_index("col")
    owned = own.shape[0] // 4
    size = w.shape[1]
    block_cols = own.shape[1] // size
    at = 0
    for dk in range(2):
        for dx in range(2):
            rows = pl.ds(pl.multiple_of((c ^ (2 * dx + dk)) * owned, owned), owned)
            for source in (own, other):
                dy[at : at + owned] = source[rows]
                at += owned
    half = keep.shape[0]
    pair = 2 * size
    for i in range(keep.shape[1] // pair):
        at = (first + 2 * i) * block_cols
        rhs = jnp.concatenate(
            [
                jnp.concatenate([w[slot_of[at + j]], w[slot_of[at + block_cols + j]]], axis=0)
                for j in range(block_cols)
            ],
            axis=1,
        )
        part = lax.dot_general(
            dy[...], rhs, (((1,), (1,)), ((), ())), preferred_element_type=jnp.float32
        ).astype(keep.dtype)
        keep[:, i * pair : (i + 1) * pair] = part[:half]
        send[:, i * pair : (i + 1) * pair] = part[half:]


def backward(first, pairs, slot_of, own, other, w, after):
    shape = pltpu.VMEM((own.shape[0], pairs * 2 * w.shape[1]), own.dtype)
    return pl.pallas_call(
        functools.partial(backward_kernel, 2 * first),
        out_shape=(shape, shape),
        in_specs=[SMEM, VMEM, VMEM, VMEM] + [ANY] * len(after),
        out_specs=(VMEM, VMEM),
        scratch_shapes=[pltpu.VMEM((2 * own.shape[0], own.shape[1]), own.dtype)],
        compiler_params=PARAMS,
        cost_estimate=pl.CostEstimate(flops=1000, bytes_accessed=1000, transcendentals=0),
    )(slot_of, own, other, resident(w), *after)


def place_kernel(counts, limits, *refs):
    y_out, dx_out = refs[-2:]
    lists = []
    for count in counts:
        lists.append(refs[:count])
        refs = refs[count:]
    r, c = lax.axis_index("row"), lax.axis_index("col")
    rows = y_out.shape[0]
    first_section = lax.axis_index("section") == 0
    for dr, pieces in enumerate(lists[:2]):
        at = (r ^ dr) * (dx_out.shape[1] // 2)
        for piece in pieces:
            token = (r * 4 + c) * rows + lax.broadcasted_iota(jnp.int32, piece.shape, 0)
            value = jnp.where(token < limits[1], piece[...].astype(jnp.float32), 0.0)
            dx_out[:, pl.ds(pl.multiple_of(at, 128), piece.shape[1])] = value.astype(dx_out.dtype)
            at += piece.shape[1]
    width = y_out.shape[1] // 4
    for dc, pieces in zip((0, 2, 1, 3), lists[2:4] + [lists[4], lists[4]]):
        at = (c ^ dc) * width
        for piece in pieces:
            value = piece[...] if dc % 2 == 0 else piece[:, dc // 2 * width : (dc // 2 + 1) * width]
            value = jnp.where(first_section, 0.0, value.astype(jnp.float32)).astype(y_out.dtype)
            y_out[:, pl.ds(pl.multiple_of(at, 128), value.shape[1])] = value
            at += value.shape[1]


def place(limits, width, lists):
    pieces = [piece for each in lists for piece in each]
    shape = jax.ShapeDtypeStruct((pieces[0].shape[0], width), pieces[0].dtype)
    return pl.pallas_call(
        functools.partial(place_kernel, [len(each) for each in lists]),
        out_shape=[shape] * 2,
        in_specs=[SMEM] + [VMEM] * len(pieces),
        out_specs=[VMEM] * 2,
        compiler_params=PARAMS,
    )(limits, *pieces)


def swap(x, axis, by):
    return lax.ppermute(x, axis, [(i, i ^ by) for i in range(lax.axis_size(axis))])


def around(x, axis, by):
    length = lax.axis_size(axis)
    return lax.ppermute(x, axis, [(i, (i + by) % length) for i in range(length)])


def tied(x, *others):
    return lax.optimization_barrier((x, *others))[0]


def added(a, b):
    return (a.astype(jnp.float32) + b.astype(jnp.float32)).astype(a.dtype)


def grid_2x4(x_fwd, dy_bwd, w_blocks, blk_row, blk_col, blk_count, tok_count, owner_order):
    token_total = x_fwd.shape[0]
    owned = token_total // 8
    slots, size = w_blocks.shape[3], w_blocks.shape[5]
    order = owner_order.reshape(-1)
    limits = tok_count.reshape(2)
    block = token_total // order.shape[0]
    w, x, slot_of = prep(
        owned,
        dy_bwd.shape[1] // size,
        blk_count.reshape(1),
        blk_row.reshape(1, slots),
        blk_col.reshape(1, slots),
        owner_order,
        w_blocks.reshape(slots, size, size),
        x_fwd,
    )
    widths = [size * 2 * share for share in F_PAIRS]
    parts = forward(block, order, limits, slot_of, x, w, widths)
    grouped = []
    for far_first in F_FAR_FIRST:
        count = 3 if far_first else 2
        grouped.append(parts[:count])
        parts = parts[count:]
    half, quarter = dy_bwd.shape[0], dy_bwd.shape[0] // 2
    made = {}

    def get(name):
        if name not in made:
            made[name] = make(name)
        return made[name]

    def make(name):
        kind, at = name[:-1], int(name[-1])
        after = [get(other)[0] for other in TIES.get(name, ())]
        if kind == "d":
            return (swap(dy_bwd, "row", 1),)
        if kind == "y":
            return (added(grouped[at][0], swap(tied(grouped[at][1], *after), "row", 1)),)
        if kind == "u":
            return (swap(tied(grouped[at][2], *after), "col", 2),)
        if kind == "v":
            far = get(f"u{at}")[0]
            return (added(far[:quarter], swap(tied(far[quarter:], *after), "row", 1)),)
        if kind == "z":
            total = get(f"y{at}")[0]
            if F_FAR_FIRST[at] == JOINT:
                far = get(f"v{at}")[0]
                total = jnp.concatenate([total[:owned], far[:owned], total[owned:], far[owned:]])
            return (around(tied(total, *after), "section", 1),)
        if kind == "w":
            return (around(tied(get(f"v{at}")[0], *after), "section", 1),)
        if kind == "fx":
            return (swap(tied(get(f"z{at}")[0][quarter:], *after), "col", 2),)
        if kind == "fc":
            near, beyond = [], []
            for part, far_first in enumerate(F_FAR_FIRST):
                here = get(f"z{part}")[0]
                if far_first == JOINT:
                    near.append(here[quarter : quarter + owned])
                    beyond.append(here[quarter + owned :])
                else:
                    near.append(here[owned:quarter])
                    beyond.append(get(f"w{part}" if far_first else f"fx{part}")[0][owned:])
            return (swap(tied(jnp.concatenate(near + beyond, axis=1), *after), "col", 1),)
        if kind == "k":
            return backward(sum(B_PAIRS[:at]), B_PAIRS[at], slot_of, dy_bwd, get("d0")[0], w, after)
        if kind == "c":
            keep, send = get(f"k{at}")
            send = tied(send, *after)
            step = send.shape[0] // C_SPLIT
            received = jnp.concatenate(
                [swap(send[i * step : (i + 1) * step], "col", 1) for i in range(C_SPLIT)]
            )
            return added(keep[quarter:], received[quarter:]), added(keep[:quarter], received[:quarter])
        if kind == "x":
            onward, kept = get(f"c{at}")
            received = swap(tied(onward, *after), "col", 2)
            return added(kept[owned:], received[owned:]), added(kept[:owned], received[:owned])
        if kind == "b":
            onward = [get(f"x{part}")[0] for part in (range(B_JOINED) if at < B_JOINED else (at,))]
            return (swap(tied(jnp.concatenate(onward, axis=1), *after), "row", 1),)

    for name in TRACE_FIRST:
        get(name)
    own, beyond = [], []
    for part, far_first in enumerate(F_FAR_FIRST):
        here = get(f"z{part}")[0]
        own.append(here[:owned])
        if far_first == JOINT:
            beyond.append(here[owned:quarter])
        else:
            beyond.append(get(f"w{part}" if far_first else f"fx{part}")[0][:owned])
    parts = range(len(B_PAIRS))
    kept = [get(f"x{part}")[1] for part in parts]
    received = [get(f"b{part}")[0] for part in parts if part == 0 or part >= B_JOINED]
    y_next, dx_section = place(limits, 4 * dy_bwd.shape[1], [kept, received, own, beyond, [get("fc0")[0]]])
    return y_next, dx_section


def passed_along(shard, axis, by):
    length = lax.axis_size(axis)
    pairs = [(i, i + by) for i in range(length) if 0 <= i + by < length]
    return lax.ppermute(shard, axis, pairs)


def any_grid(x_fwd, dy_bwd, w_blocks, blk_row, blk_col, blk_count, tok_count, owner_order):
    row_count = lax.axis_size("row")
    col_count = lax.axis_size("col")
    token_total, in_width = x_fwd.shape
    out_width = dy_bwd.shape[1]
    slot_total = w_blocks.shape[3]
    block_size = w_blocks.shape[5]
    block_rows = in_width // block_size
    block_cols = out_width // block_size
    owned_rows = token_total // (row_count * col_count)
    weights = w_blocks.reshape(slot_total, block_size, block_size)
    live = (jnp.arange(slot_total) < blk_count.reshape(())).astype(weights.dtype)
    dense_blocks = jnp.zeros((block_rows, block_cols, block_size, block_size), weights.dtype)
    dense_blocks = dense_blocks.at[blk_row.reshape(slot_total), blk_col.reshape(slot_total)].add(
        weights * live[:, None, None]
    )
    dense_weight = jnp.transpose(dense_blocks, (0, 2, 1, 3)).reshape(in_width, out_width)
    limits = tok_count.reshape(2)
    block_total = owner_order.shape[1]
    block_length = token_total // block_total
    token_index = (
        owner_order.reshape(block_total)[:, None] * block_length + jnp.arange(block_length)[None, :]
    ).reshape(token_total)
    ordered_rows = jnp.take(x_fwd, token_index, axis=0)
    ordered_rows = jnp.where(
        (token_index < limits[0])[:, None], ordered_rows, jnp.zeros_like(ordered_rows)
    )
    partial_value = jnp.dot(ordered_rows, dense_weight, preferred_element_type=jnp.float32).astype(
        jnp.bfloat16
    )
    outgoing = partial_value.reshape(row_count * col_count, owned_rows, out_width)
    received = lax.all_to_all(outgoing, ("row", "col"), split_axis=0, concat_axis=2, tiled=True)
    summed = received.reshape(owned_rows, row_count, col_count * out_width).astype(jnp.float32)
    forward_act = jnp.sum(summed, axis=1).astype(jnp.bfloat16)
    y_next = passed_along(forward_act, "section", 1)
    grad_rows = dy_bwd.shape[0]
    grad_index = lax.axis_index("row") * grad_rows + jnp.arange(grad_rows)
    grad_kept = jnp.where((grad_index < limits[1])[:, None], dy_bwd, jnp.zeros_like(dy_bwd))
    grad_partial = lax.dot_general(
        lax.all_gather(grad_kept, "row", axis=0, tiled=True),
        dense_weight,
        (((1,), (1,)), ((), ())),
        preferred_element_type=jnp.float32,
    ).astype(jnp.bfloat16)
    grad_outgoing = grad_partial.reshape(row_count * col_count, owned_rows, in_width)
    grad_received = lax.all_to_all(
        grad_outgoing, ("row", "col"), split_axis=0, concat_axis=2, tiled=True
    )
    grad_summed = grad_received.reshape(owned_rows, row_count, col_count, in_width).astype(
        jnp.float32
    )
    dx_section = (
        jnp.sum(grad_summed, axis=2).reshape(owned_rows, row_count * in_width).astype(jnp.bfloat16)
    )
    return (y_next, dx_section)


def solution(mesh):
    small = mesh.shape["row"] == 2 and mesh.shape["col"] == 4
    return jax.shard_map(
        grid_2x4 if small else any_grid,
        mesh=mesh,
        in_specs=(
            P("section", "row"),
            P(("section", "row"), "col"),
            P("section", "row", "col", None, None, None),
            P("section", "row", "col", None),
            P("section", "row", "col", None),
            P("section", "row", "col"),
            P("section", None),
            P("section", None),
        ),
        out_specs=(P(("section", "row", "col"), None), P(("section", "row", "col"), None)),
        check_vma=False,
    )
```
